128 devices in a mesh: dp: 32 (over z, x, core), sy: 2 (over y_hi), sx: 2 (over y_lo).
Axes of the slice: x: 4, y: 4 (y_hi: 2, y_lo: 2; y = y_hi * 2 + y_lo), z: 4, core: 2. Of those that a mesh axis runs over, the one named last changes fastest.
Arguments:
- features: bfloat16 [32, 16, 32, 640], P('dp', 'sy', 'sx'), may hold values from -6 to 6
- bucket_ids: int32 [32], P('dp'), may hold values from 0 to 7
- bucket_sizes: int32 [8, 2], replicated, may hold values from 8 to 32, as said below
- conv_weight: bfloat16 [5760, 640], replicated, may hold values from -0.078125 to 0.078125
- norm_gain: float32 [640], replicated, may hold values from 0.25 to 1.75
- query_weight: bfloat16 [640, 640], replicated, may hold values from -0.25 to 0.25
- key_weight: bfloat16 [640, 640], replicated, may hold values from -0.25 to 0.25
- value_weight: bfloat16 [640, 640], replicated, may hold values from -0.25 to 0.25
- out_weight: bfloat16 [640, 640], replicated, may hold values from -0.25 to 0.25
- out_grad: bfloat16 [32, 16, 32, 640], P('dp', 'sy', 'sx'), may hold values from -6 to 6
Outputs:
- block_out: bfloat16 [32, 16, 32, 640], P('dp', 'sy', 'sx')
- grad_conv: float32 [5760, 640], P('dp', ('sy', 'sx'))
- grad_query: float32 [640, 640], P('dp', ('sy', 'sx'))
- grad_key: float32 [640, 640], P('dp', ('sy', 'sx'))
- grad_value: float32 [640, 640], P('dp', ('sy', 'sx'))
- grad_out: float32 [640, 640], P('dp', ('sy', 'sx'))
The draws below stay inside these ranges and needn't reach their ends.
Inputs may be any that keep to these rules, and one draw needn't show every extreme that they name: Each row of bucket_sizes holds a bucket's latent rows, from 8 to 16, and columns, from 16 to 32; bucket 0 is the full 16 x 32 grid and bucket 1 is 8 x 16.
All inputs are finite; a program needn't handle non-finite values.
Results may differ from the reference program's by a relative error of at most 0.013.
Values may be sent and summed in bfloat16 or wider, within the bound.
No kernel may reach another device: no remote copies, remote signals or barrier semaphores. Data moves between devices by JAX's collectives and lax.ppermute only.
A program may use at most 192 MiB of HBM per device.

```python
import jax
import jax.numpy as jnp
from jax import lax

C = 640
HEADS = 10
BUCKETS = 8
HG = 16
WG = 32
IMAGES = 32


def draw_bucket_sizes(key, part):
    first = jax.random.fold_in(key, 11)
    second = jax.random.fold_in(key, 23)
    heights = jax.random.randint(first, (BUCKETS, 1), HG // 2, HG + 1, dtype=jnp.int32)
    widths = jax.random.randint(second, (BUCKETS, 1), WG // 2, WG + 1, dtype=jnp.int32)
    sizes = jnp.concatenate([heights, widths], axis=1)
    sizes = sizes.at[0, 0].set(HG).at[0, 1].set(WG)
    sizes = sizes.at[1, 0].set(HG // 2).at[1, 1].set(WG // 2)
    return sizes


def touch_ends(entries, rng, least, largest):
    longest = entries.shape.index(max(entries.shape))
    spots = []
    for shift in (0, 1):
        where = [jax.random.randint(jax.random.fold_in(rng, axis), (), 0, length) for axis, length in enumerate(entries.shape)]
        where[longest] = (where[longest] + shift) % entries.shape[longest]
        spots.append(tuple(where))
    return entries.at[spots[0]].set(least).at[spots[1]].set(largest)


def level_of(stream_key, dims, split, low, high):
    def one(position, blocks):
        steps = jax.random.uniform(jax.random.fold_in(jax.random.fold_in(stream_key, 6), position), (blocks,), jnp.float32, low / len(split), high / len(split))
        return jnp.repeat(jnp.exp(steps), dims[position] // blocks).reshape((-1,) + (1,) * (len(dims) - position - 1))

    loudness = one(*split[0])
    for cut in split[1:]:
        loudness = loudness * one(*cut)
    return loudness


def bell_draw(rng, dims, deviation, limit, pieces=(), kind=jnp.bfloat16):
    level = level_of(rng, dims, pieces, -0.22, 0.18) if pieces else 1.0
    array = jax.random.normal(rng, dims, jnp.float32) * deviation * level
    return jnp.minimum(jnp.maximum(array, -limit), limit).astype(kind)


def setup_inputs(seed: int = 0) -> dict:
    key_of = jax.random.split(jax.random.key(seed), 11)
    return {
        "features": bell_draw(key_of[0], (IMAGES, HG, WG, C), 1.0, 6.0, ((0, 32), (1, 2), (2, 2))),
        "bucket_ids": touch_ends(jax.random.randint(key_of[1], (IMAGES,), 0, BUCKETS), jax.random.fold_in(key_of[1], 1), 0, BUCKETS - 1).astype(jnp.int32),
        "bucket_sizes": draw_bucket_sizes(jax.random.fold_in(key_of[10], 71), 0),
        "conv_weight": bell_draw(key_of[3], (9 * C, C), (9 * C) ** -0.5, 0.078125),
        "norm_gain": jnp.clip(1.0 + 0.15 * jax.random.normal(key_of[4], (C,), jnp.float32), 0.25, 1.75),
        "query_weight": bell_draw(key_of[5], (C, C), C ** -0.5, 0.25),
        "key_weight": bell_draw(key_of[6], (C, C), C ** -0.5, 0.25),
        "value_weight": bell_draw(key_of[7], (C, C), C ** -0.5, 0.25),
        "out_weight": bell_draw(key_of[8], (C, C), C ** -0.5, 0.25),
        "out_grad": bell_draw(key_of[9], (IMAGES, HG, WG, C), 1.0, 6.0, ((0, 32), (1, 2), (2, 2))),
    }


def layer_norm(hidden, gain):
    mean = lax.optimization_barrier(jnp.mean(hidden, axis=-1, keepdims=True))
    centred = hidden - mean
    spread = lax.optimization_barrier(jnp.mean(centred * centred, axis=-1, keepdims=True))
    return centred * lax.rsqrt(spread + 1e-05) * gain.astype(jnp.float32)

def patch_rows(padded, rows, cols):
    taps = [padded[dy:dy + rows, dx:dx + cols, :] for dy in range(3) for dx in range(3)]
    return jnp.concatenate(taps, axis=-1).reshape(rows * cols, -1)

def head_probs(query, keys, key_valid, start, width, scale):
    scores = jnp.dot(query[:, start:start + width], keys[:, start:start + width].T, preferred_element_type=jnp.float32) * scale
    scores = jnp.where(key_valid[None, :], scores, -1e+30)
    return jax.nn.softmax(scores, axis=-1)

def attend(query, keys, values, key_valid, heads):
    width = query.shape[1] // heads
    scale = width ** (-0.5)
    parts = []
    for head in range(heads):
        start = head * width
        probs = head_probs(query, keys, key_valid, start, width, scale)
        parts.append(jnp.dot(probs.astype(jnp.bfloat16), values[:, start:start + width], preferred_element_type=jnp.float32).astype(jnp.bfloat16))
    return jnp.concatenate(parts, axis=-1)

def attend_back(query, keys, values, key_valid, grad_context, heads):
    width = query.shape[1] // heads
    scale = width ** (-0.5)
    dq_parts, dk_parts, dv_parts = ([], [], [])
    for head in range(heads):
        start = head * width
        probs = head_probs(query, keys, key_valid, start, width, scale)
        probs_b = probs.astype(jnp.bfloat16)
        grad_slice = grad_context[:, start:start + width]
        dprob = jnp.dot(grad_slice, values[:, start:start + width].T, preferred_element_type=jnp.float32)
        delta = lax.optimization_barrier(jnp.sum(probs * dprob, axis=-1, keepdims=True))
        dscore = (probs * (dprob - delta) * scale).astype(jnp.bfloat16)
        dq_parts.append(jnp.dot(dscore, keys[:, start:start + width], preferred_element_type=jnp.float32))
        dk_parts.append(jnp.dot(dscore.T, query[:, start:start + width], preferred_element_type=jnp.float32))
        dv_parts.append(jnp.dot(probs_b.T, grad_slice, preferred_element_type=jnp.float32))
    return (jnp.concatenate(dq_parts, axis=-1), jnp.concatenate(dk_parts, axis=-1), jnp.concatenate(dv_parts, axis=-1))

def reference(features, bucket_ids, bucket_sizes, conv_weight, norm_gain, query_weight, key_weight, value_weight, out_weight, out_grad):
    width = features.shape[3]

    def one_image(totals, items):
        feats, bucket, cotangent = items
        chosen = jnp.arange(BUCKETS, dtype=jnp.int32) == bucket
        height = jnp.sum(jnp.where(chosen, bucket_sizes[:, 0], 0))
        breadth = jnp.sum(jnp.where(chosen, bucket_sizes[:, 1], 0))
        valid = (jnp.arange(HG, dtype=jnp.int32)[:, None] < height) & (jnp.arange(WG, dtype=jnp.int32)[None, :] < breadth)
        valid_flat = valid.reshape(-1, 1).astype(jnp.float32)
        key_valid = valid.reshape(-1)
        xin = (feats.astype(jnp.float32) * valid[:, :, None].astype(jnp.float32)).astype(jnp.bfloat16)
        padded = jnp.pad(xin, ((1, 1), (1, 1), (0, 0)))
        patches = patch_rows(padded, HG, WG)
        pre = jnp.dot(patches, conv_weight, preferred_element_type=jnp.float32)
        hidden = (valid_flat * (xin.reshape(-1, width).astype(jnp.float32) + jax.nn.silu(pre))).astype(jnp.bfloat16)
        hidden_f = hidden.astype(jnp.float32)
        normed_f, pullback = jax.vjp(lambda value: layer_norm(value, norm_gain), hidden_f)
        normed = normed_f.astype(jnp.bfloat16)
        query = jnp.dot(normed, query_weight, preferred_element_type=jnp.float32).astype(jnp.bfloat16)
        keys = jnp.dot(normed, key_weight, preferred_element_type=jnp.float32).astype(jnp.bfloat16)
        values = jnp.dot(normed, value_weight, preferred_element_type=jnp.float32).astype(jnp.bfloat16)
        context = attend(query, keys, values, key_valid, HEADS)
        block = (valid_flat * (hidden_f + jnp.dot(context, out_weight, preferred_element_type=jnp.float32))).astype(jnp.bfloat16)
        grad_b = (cotangent.reshape(-1, width).astype(jnp.float32) * valid_flat).astype(jnp.bfloat16)
        grad_wo = jnp.dot(context.T, grad_b, preferred_element_type=jnp.float32)
        grad_context = jnp.dot(grad_b, out_weight.T, preferred_element_type=jnp.float32).astype(jnp.bfloat16)
        dquery, dkey, dvalue = attend_back(query, keys, values, key_valid, grad_context, HEADS)
        dquery = dquery.astype(jnp.bfloat16)
        dkey = dkey.astype(jnp.bfloat16)
        dvalue = dvalue.astype(jnp.bfloat16)
        grad_wq = jnp.dot(normed.T, dquery, preferred_element_type=jnp.float32)
        grad_wk = jnp.dot(normed.T, dkey, preferred_element_type=jnp.float32)
        grad_wv = jnp.dot(normed.T, dvalue, preferred_element_type=jnp.float32)
        dnormed = jnp.dot(dquery, query_weight.T, preferred_element_type=jnp.float32)
        dnormed = dnormed + jnp.dot(dkey, key_weight.T, preferred_element_type=jnp.float32)
        dnormed = dnormed + jnp.dot(dvalue, value_weight.T, preferred_element_type=jnp.float32)
        dhidden = grad_b.astype(jnp.float32) + pullback(dnormed)[0]
        sig = jax.nn.sigmoid(pre)
        dpre = (valid_flat * dhidden * sig * (1.0 + pre * (1.0 - sig))).astype(jnp.bfloat16)
        grad_cv = jnp.dot(patches.T, dpre, preferred_element_type=jnp.float32)
        totals = (totals[0] + grad_cv, totals[1] + grad_wq, totals[2] + grad_wk, totals[3] + grad_wv, totals[4] + grad_wo)
        return (totals, block.reshape(HG, WG, width))
    square = jnp.zeros((width, width), jnp.float32)
    start = (jnp.zeros((9 * width, width), jnp.float32), square, square, square, square)
    totals, blocks = lax.scan(one_image, start, (features, bucket_ids, out_grad))
    return (blocks, totals[0], totals[1], totals[2], totals[3], totals[4])
```

```python
import jax
import jax.numpy as jnp
from jax import lax
from jax.experimental import pallas as pl
from jax.experimental.pallas import tpu as pltpu
from jax.sharding import PartitionSpec as P

HEADS = 10
EPS = 1e-05
ROWS, COLS, CH = 16, 32, 640
CELLS = ROWS * COLS
TILE_ROWS, TILE_COLS = 8, 16
WIDTH = CH // HEADS
PART = CH // 4
MAIN, REST = 128, 32
PIECES = 32
CONV_ROWS = 9 * CH // PIECES
QUARTER = CONV_ROWS // 4
PROJ_ROWS = CH // PIECES
AT_PROJ_REST = 4 * PROJ_ROWS
AT_CONV = 112
AT_CONV_REST = 304
PIECE = 352

f32 = jnp.float32
bf16 = jnp.bfloat16


def dot(a, b):
    return jnp.dot(a, b, preferred_element_type=f32)


def dot_t(a, b):
    return lax.dot_general(a, b, (((1,), (1,)), ((), ())), preferred_element_type=f32)


def iota(shape, dim):
    return lax.broadcasted_iota(jnp.int32, shape, dim)


def valid_rows(meta, start, count):
    cell = start + iota((count, 1), 0)
    return ((cell >> 5) < meta[0]) & ((cell & 31) < meta[1])


def tile_row(ref, r):
    base = (r >> 3) * (2 * TILE_ROWS * TILE_COLS) + (r & 7) * TILE_COLS
    left = ref[pl.ds(pl.multiple_of(base, 16), 16), :]
    right = ref[pl.ds(pl.multiple_of(base + TILE_ROWS * TILE_COLS, 16), 16), :]
    return jnp.concatenate([left, right], axis=0)


def front_kernel(
    meta, xg, conv_hbm, gain, wq_hbm, wk_hbm, wv_hbm,
    xin_o, pre_o, hid_o, nrm_o, q_o, k_o, v_o,
    taps, conv, proj, sems,
):
    third = 3 * CH
    copies = [
        pltpu.make_async_copy(
            conv_hbm.at[pl.ds(i * third, third)], conv.at[pl.ds(i * third, third)], sems.at[i]
        )
        for i in range(3)
    ]
    copies += [
        pltpu.make_async_copy(w, proj.at[i], sems.at[3 + i])
        for i, w in enumerate((wq_hbm, wk_hbm, wv_hbm))
    ]
    for copy in copies:
        copy.start()
    taps[0:COLS, :] = jnp.zeros((COLS, third), bf16)
    taps[CELLS + COLS :, :] = jnp.zeros((COLS, third), bf16)
    col = iota((COLS, 1), 0)

    def place(r, carry):
        x = tile_row(xg, r).astype(f32)
        x = jnp.where((r < meta[0]) & (col < meta[1]), x, 0.0)
        xb = x.astype(bf16)
        at = pl.multiple_of(r * COLS, COLS)
        xin_o[pl.ds(at, COLS), :] = xb
        to = pl.ds(at + COLS, COLS)
        taps[to, 0:CH] = jnp.where(col == 0, 0.0, pltpu.roll(x, 1, 0)).astype(bf16)
        taps[to, CH : 2 * CH] = xb
        taps[to, 2 * CH :] = jnp.where(col == COLS - 1, 0.0, pltpu.roll(x, COLS - 1, 0)).astype(bf16)
        return carry

    lax.fori_loop(0, ROWS, place, 0)
    for dy in range(3):
        copies[dy].wait()
        part = dot(taps[dy * COLS : dy * COLS + CELLS, :], conv[dy * third : (dy + 1) * third, :])
        if dy == 0:
            pre_o[...] = part
        else:
            pre_o[...] += part

    step = 64

    def norm(i, carry):
        at = pl.multiple_of(i * step, step)
        rows = pl.ds(at, step)
        pre = pre_o[rows, :]
        act = pre / (1.0 + jnp.exp(-pre))
        hid = jnp.where(valid_rows(meta, at, step), xin_o[rows, :].astype(f32) + act, 0.0)
        hid = hid.astype(bf16)
        hid_o[rows, :] = hid
        hid = hid.astype(f32)
        centred = hid - jnp.mean(hid, axis=1, keepdims=True)
        spread = jnp.mean(centred * centred, axis=1, keepdims=True)
        nrm_o[rows, :] = (centred * lax.rsqrt(spread + EPS) * gain[...]).astype(bf16)
        return carry

    lax.fori_loop(0, CELLS // step, norm, 0)
    for copy in copies[3:]:
        copy.wait()
    nrm = nrm_o[...]
    q_o[...] = (dot(nrm, proj[0]).astype(bf16).astype(f32) * (WIDTH**-0.5)).astype(bf16)
    k_o[...] = dot(nrm, proj[1]).astype(bf16)
    v_o[...] = dot(nrm, proj[2]).astype(bf16)


def back_kernel(
    meta, og, xin, hid, nrm, pre, q, k, v, gain, wq, wk, wv, wo,
    blk_o, mine_o, theirs_o,
    gb, gc, kt, vt, ctxt, dqt, dk, dv, bias, dn, dpre, wide, padm, padr, gmain, grest, gproj, stage, half,
):
    sy, sx, core = meta[2], meta[3], meta[4]
    col = iota((COLS, 1), 0)

    def place(r, carry):
        g = tile_row(og, r)
        g = jnp.where((r < meta[0]) & (col < meta[1]), g, jnp.zeros_like(g))
        gb[pl.ds(pl.multiple_of(r * COLS, COLS), COLS), :] = g
        return carry

    lax.fori_loop(0, ROWS, place, 0)
    gc[...] = dot_t(gb[...], wo[...]).astype(bf16)
    kt[...] = k[...].T
    vt[...] = v[...].T
    lane = iota((1, 2 * WIDTH), 1)
    ok = valid_rows(meta, 0, CELLS)
    for e in range(2):
        bias[e] = jnp.where((lane == WIDTH * (1 - e)) & ~ok, -1e30, 0.0).astype(bf16)
    block = 256

    def pair(hp, carry):
        lanes = pl.ds(pl.multiple_of(hp * 2 * WIDTH, 2 * WIDTH), 2 * WIDTH)
        k2 = k[:, lanes]
        v2 = v[:, lanes]
        dk2 = jnp.zeros((CELLS, 2 * WIDTH), f32)
        dv2 = jnp.zeros((CELLS, 2 * WIDTH), f32)
        for e in range(2):
            own = (lane >= WIDTH * e) & (lane < WIDTH * (e + 1))
            ka = jnp.where(own, k2, bias[e])
            rows = pl.ds(pl.multiple_of(hp * 2 * WIDTH + e * WIDTH, WIDTH), WIDTH)
            for qb in range(CELLS // block):
                cells = slice(qb * block, (qb + 1) * block)
                q2 = q[cells, lanes]
                g2 = gc[cells, lanes]
                qm = jnp.where(own, q2, jnp.zeros_like(q2))
                gm = jnp.where(own, g2, jnp.zeros_like(g2))
                one = jnp.where(lane == WIDTH * (1 - e), 1.0, 0.0).astype(bf16)
                qa = jnp.where(own, q2, one)
                s = dot_t(ka, qa)
                ex = jnp.exp(s - jnp.max(s, axis=0, keepdims=True))
                p = ex * (1.0 / jnp.sum(ex, axis=0, keepdims=True))
                pb = p.astype(bf16)
                ctxt[rows, cells] = dot(vt[rows, :], pb).astype(bf16)
                dp = dot_t(v2, gm)
                delta = jnp.sum(p * dp, axis=0, keepdims=True)
                ds = (p * (dp - delta)).astype(bf16)
                dqt[rows, cells] = (dot(kt[rows, :], ds) * (WIDTH**-0.5)).astype(bf16)
                dk2 = dk2 + dot(ds, qm)
                dv2 = dv2 + dot(pb, gm)
        dk[:, lanes] = dk2.astype(bf16)
        dv[:, lanes] = dv2.astype(bf16)
        return carry

    lax.fori_loop(0, HEADS // 2, pair, 0)

    part = CELLS // 2
    at = pl.multiple_of(sy * part, part)
    ctx_half = ctxt[:, pl.ds(at, part)].T
    half[...] = hid[pl.ds(at, part), :].astype(f32) + dot(ctx_half, wo[...])
    for r in range(TILE_ROWS):
        rows = half[pl.ds(pl.multiple_of(r * COLS + sx * TILE_COLS, 16), TILE_COLS), :]
        cells = sx * TILE_COLS + iota((TILE_COLS, 1), 0)
        keep = (sy * TILE_ROWS + r < meta[0]) & (cells < meta[1])
        blk_o[r * TILE_COLS : (r + 1) * TILE_COLS, :] = jnp.where(keep, rows, 0.0).astype(bf16)

    dq = dqt[...].T
    dn[...] = dot_t(dq, wq[...]) + dot_t(dk[...], wk[...]) + dot_t(dv[...], wv[...])
    step = 64

    def norm_back(i, carry):
        at = pl.multiple_of(i * step, step)
        rows = pl.ds(at, step)
        h = hid[rows, :].astype(f32)
        centred = h - jnp.mean(h, axis=1, keepdims=True)
        rstd = lax.rsqrt(jnp.mean(centred * centred, axis=1, keepdims=True) + EPS)
        xhat = centred * rstd
        dx = dn[rows, :] * gain[...]
        m1 = jnp.mean(dx, axis=1, keepdims=True)
        m2 = jnp.mean(dx * xhat, axis=1, keepdims=True)
        dh = gb[rows, :].astype(f32) + rstd * (dx - m1 - xhat * m2)
        a = pre[rows, :]
        sig = 1.0 / (1.0 + jnp.exp(-a))
        out = dh * sig * (1.0 + a * (1.0 - sig))
        dpre[rows, :] = jnp.where(valid_rows(meta, at, step), out, 0.0).astype(bf16)
        return carry

    lax.fori_loop(0, CELLS // step, norm_back, 0)

    first = (sy * 2 + sx) * PART
    row = iota((CH, 1), 0) - first

    def pick(lo, lanes, group=None):
        n = iota((1, lanes), 1)
        want = n + lo if group is None else (n & (REST - 1)) + lo
        hit = row == want
        if group is not None and group >= 0:
            hit = hit & ((n >> 5) == group)
        return jnp.where(hit, 1.0, 0.0).astype(bf16)

    nt = nrm[...].T
    main = pick(0, MAIN)
    grads = (dq, dk[...], dv[...], gb[...])
    mains, rests = [], []
    for w, g in enumerate(grads):
        both = dot(g, jnp.concatenate([main, pick(MAIN, 4 * REST, w)], axis=1))
        mains.append(both[:, :MAIN].astype(bf16))
        rests.append(both[:, MAIN:])
    qkv = dot(nt, jnp.concatenate(mains[:3] + [(rests[0] + rests[1] + rests[2]).astype(bf16)], axis=1))
    out = dot(ctxt[...], jnp.concatenate([mains[3], rests[3].astype(bf16)], axis=1))
    for w in range(3):
        gproj[w * CH : (w + 1) * CH, :] = qkv[:, w * MAIN : (w + 1) * MAIN]
    gproj[3 * CH : 4 * CH, :] = out[:, :MAIN]
    gproj[4 * CH :, :] = qkv[:, 3 * MAIN :] + out[:, MAIN:]

    ccol = iota((CELLS, 1), 0) & (COLS - 1)
    dmain = dot(dpre[...], main)
    drest = dot(dpre[...], pick(MAIN, 3 * MAIN, -1))
    up = lambda x: jnp.where(ccol == COLS - 1, 0.0, pltpu.roll(x, CELLS - 1, 0))
    down = lambda x: jnp.where(ccol == 0, 0.0, pltpu.roll(x, 1, 0))
    padm[...] = jnp.zeros_like(padm)
    padr[...] = jnp.zeros_like(padr)
    inner = slice(COLS, COLS + CELLS)
    padm[0, inner, :] = up(dmain).astype(bf16)
    padm[1, inner, :] = dmain.astype(bf16)
    padm[2, inner, :] = down(dmain).astype(bf16)
    tap = iota((1, 3 * MAIN), 1) >> 5
    tap_dx = tap % 3
    tap_dy = tap // 3
    padr[inner, :] = jnp.where(tap_dx == 0, up(drest), jnp.where(tap_dx == 1, drest, down(drest)))
    for t in range(9):
        lo = (2 - t // 3) * COLS
        wide[:, t * MAIN : (t + 1) * MAIN] = padm[t % 3, lo : lo + CELLS, :]
    wide[:, 9 * MAIN :] = jnp.where(
        tap_dy == 0,
        padr[2 * COLS :, :],
        jnp.where(tap_dy == 1, padr[inner, :], padr[0:CELLS, :]),
    ).astype(bf16)
    xt = xin[...].T
    for j in range(6):
        g = dot(xt, wide[:, j * 256 : (j + 1) * 256])
        for i in range(2):
            t = 2 * j + i
            val = g[:, i * MAIN : (i + 1) * MAIN]
            if t < 9:
                gmain[t * CH : (t + 1) * CH, :] = val
            else:
                for u in range(4):
                    n = (t - 9) * 4 + u
                    if n < 9:
                        grest[n * CH : (n + 1) * CH, 0:REST] = val[:, u * REST : (u + 1) * REST]

    stage[...] = jnp.zeros_like(stage)
    for j in range(PIECES // 2):
        for c in range(2):
            d = 2 * j + c
            for w in range(4):
                stage[c, w * PROJ_ROWS : (w + 1) * PROJ_ROWS, :] = gproj[
                    w * CH + d * PROJ_ROWS : w * CH + (d + 1) * PROJ_ROWS, :
                ]
            stage[c, AT_PROJ_REST : AT_PROJ_REST + PROJ_ROWS, :] = gproj[
                4 * CH + d * PROJ_ROWS : 4 * CH + (d + 1) * PROJ_ROWS, :
            ]
            stage[c, AT_CONV : AT_CONV + CONV_ROWS, :] = gmain[d * CONV_ROWS : (d + 1) * CONV_ROWS, :]
            stage[c, AT_CONV_REST : AT_CONV_REST + QUARTER, :] = jnp.concatenate(
                [
                    grest[d * CONV_ROWS + g * QUARTER : d * CONV_ROWS + (g + 1) * QUARTER, 0:REST]
                    for g in range(4)
                ],
                axis=1,
            )
        zero, one = stage[0], stage[1]
        mine_o[j] = jnp.where(core == 0, zero, one).astype(bf16)
        theirs_o[j] = jnp.where(core == 0, one, zero).astype(bf16)


def last_kernel(pieces, conv_o, q_o, k_o, v_o, o_o, total):
    acc = pieces[0].astype(f32)
    for j in range(1, pieces.shape[0]):
        acc = acc + pieces[j].astype(f32)
    total[...] = acc
    conv_o[:, :MAIN] = total[AT_CONV : AT_CONV + CONV_ROWS, :]
    for g in range(4):
        conv_o[g * QUARTER : (g + 1) * QUARTER, MAIN:] = total[
            AT_CONV_REST : AT_CONV_REST + QUARTER, g * REST : (g + 1) * REST
        ]
    for w, out in enumerate((q_o, k_o, v_o, o_o)):
        out[:, :MAIN] = total[w * PROJ_ROWS : (w + 1) * PROJ_ROWS, :]
        out[:, MAIN:] = total[AT_PROJ_REST : AT_PROJ_REST + PROJ_ROWS, w * REST : (w + 1) * REST]


VM = pl.BlockSpec(memory_space=pltpu.VMEM)
SM = pl.BlockSpec(memory_space=pltpu.SMEM)
AN = pl.BlockSpec(memory_space=pl.ANY)


def shape(dims, dtype):
    return jax.ShapeDtypeStruct(dims, dtype)


def front(meta, xg, conv_weight, gain, wq, wk, wv):
    flat = (CELLS, CH)
    return pl.pallas_call(
        front_kernel,
        name="front",
        out_shape=[shape(flat, bf16), shape(flat, f32)] + [shape(flat, bf16)] * 5,
        in_specs=[SM, VM, AN, VM, AN, AN, AN],
        out_specs=[VM] * 7,
        scratch_shapes=[
            pltpu.VMEM((CELLS + 2 * COLS, 3 * CH), bf16),
            pltpu.VMEM((9 * CH, CH), bf16),
            pltpu.VMEM((3, CH, CH), bf16),
            pltpu.SemaphoreType.DMA((6,)),
        ],
        compiler_params=pltpu.CompilerParams(vmem_limit_bytes=40 * 2**20),
    )(meta, xg, conv_weight, gain, wq, wk, wv)


def back(meta, og, xin, hid, nrm, pre, q, k, v, gain, wq, wk, wv, wo):
    flat, turned = (CELLS, CH), (CH, CELLS)
    return pl.pallas_call(
        back_kernel,
        name="back",
        out_shape=[
            shape((TILE_ROWS * TILE_COLS, CH), bf16),
            shape((PIECES // 2, PIECE, 128), bf16),
            shape((PIECES // 2, PIECE, 128), bf16),
        ],
        in_specs=[SM] + [VM] * 13,
        out_specs=[VM] * 3,
        scratch_shapes=[
            pltpu.VMEM(flat, bf16),
            pltpu.VMEM(flat, bf16),
            pltpu.VMEM(turned, bf16),
            pltpu.VMEM(turned, bf16),
            pltpu.VMEM(turned, bf16),
            pltpu.VMEM(turned, bf16),
            pltpu.VMEM(flat, bf16),
            pltpu.VMEM(flat, bf16),
            pltpu.VMEM((2, CELLS, 128), bf16),
            pltpu.VMEM(flat, f32),
            pltpu.VMEM(flat, bf16),
            pltpu.VMEM((CELLS, 12 * 128), bf16),
            pltpu.VMEM((3, CELLS + 2 * COLS, 128), bf16),
            pltpu.VMEM((CELLS + 2 * COLS, 3 * 128), f32),
            pltpu.VMEM((9 * CH, 128), f32),
            pltpu.VMEM((9 * CH, 128), f32),
            pltpu.VMEM((5 * CH, 128), f32),
            pltpu.VMEM((2, PIECE, 128), f32),
            pltpu.VMEM((CELLS // 2, CH), f32),
        ],
        compiler_params=pltpu.CompilerParams(vmem_limit_bytes=50 * 2**20),
    )(meta, og, xin, hid, nrm, pre, q, k, v, gain, wq, wk, wv, wo)


def last(pieces):
    small = shape((PROJ_ROWS, PART), f32)
    return pl.pallas_call(
        last_kernel,
        name="last",
        out_shape=[shape((CONV_ROWS, PART), f32), small, small, small, small],
        in_specs=[VM],
        out_specs=[VM] * 5,
        scratch_shapes=[pltpu.VMEM((PIECE, 128), f32)],
    )(pieces)


def body(
    features, bucket_ids, bucket_sizes, conv_weight, norm_gain,
    query_weight, key_weight, value_weight, out_weight, out_grad,
):
    chosen = jnp.arange(bucket_sizes.shape[0], dtype=jnp.int32) == bucket_ids[0]
    size = jnp.sum(jnp.where(chosen[:, None], bucket_sizes, 0), axis=0)
    core = lax.axis_index("dp") % 2
    meta = jnp.stack([size[0], size[1], lax.axis_index("sy"), lax.axis_index("sx"), core])
    meta = meta.astype(jnp.int32)
    gain = norm_gain.reshape(1, CH)
    tiles = ("sy", "sx")
    xg = lax.all_gather(features.reshape(-1, CH), tiles, axis=0, tiled=True)
    og = lax.all_gather(out_grad.reshape(-1, CH), tiles, axis=0, tiled=True)
    xin, pre, hid, nrm, q, k, v = front(
        meta, xg, conv_weight, gain, query_weight, key_weight, value_weight
    )
    block, mine, theirs = back(
        meta, og, xin, hid, nrm, pre, q, k, v, gain,
        query_weight, key_weight, value_weight, out_weight,
    )
    count = lax.axis_size("dp")
    other = lax.ppermute(theirs, "dp", [(i, i ^ 1) for i in range(count)])
    both = (mine.astype(f32) + other.astype(f32)).astype(bf16)
    groups = [[c + 2 * i for i in range(count // 2)] for c in range(2)]
    pieces = lax.all_to_all(both, "dp", 0, 0, tiled=True, axis_index_groups=groups)
    grads = last(pieces)
    return (block.reshape(features.shape), *grads)


def solution(mesh):
    tiles = P("dp", "sy", "sx", None)
    grad = P("dp", ("sy", "sx"))
    return jax.shard_map(
        body,
        mesh=mesh,
        in_specs=(tiles, P("dp"), P(), P(), P(), P(), P(), P(), P(), tiles),
        out_specs=(tiles, grad, grad, grad, grad, grad),
        check_vma=False,
    )
```

```python
import jax
import jax.numpy as jnp
from jax import lax
from jax.experimental import pallas as pl
from jax.experimental.pallas import tpu as pltpu
from jax.sharding import PartitionSpec as P

HEADS = 10
EPS = 1e-05
LOG2E = 1.4426950408889634
SLOT = 64 + 16
ROWS, COLS, CH = 16, 32, 640
CELLS = ROWS * COLS
TILE_ROWS, TILE_COLS = 8, 16
WIDTH = CH // HEADS
PART = CH // 4
MAIN, REST = 128, 32
PIECES = 32
CONV_ROWS = 9 * CH // PIECES
QUARTER = CONV_ROWS // 4
PROJ_ROWS = CH // PIECES
AT_PROJ_REST = 4 * PROJ_ROWS
AT_CONV = 112
AT_CONV_REST = 304
PIECE = 352

f32 = jnp.float32
bf16 = jnp.bfloat16


def dot(a, b):
    return jnp.dot(a, b, preferred_element_type=f32)


def dot_t(a, b):
    return lax.dot_general(a, b, (((1,), (1,)), ((), ())), preferred_element_type=f32)


def iota(shape, dim):
    return lax.broadcasted_iota(jnp.int32, shape, dim)


def valid_rows(meta, start, count):
    cell = start + iota((count, 1), 0)
    return ((cell >> 5) < meta[0]) & ((cell & 31) < meta[1])


def place_tiles(meta, tiles, out):
    edge = iota((TILE_COLS, 1), 0)
    for shift, ref in enumerate(tiles):
        tile = (meta[2] * 2 + meta[3] - shift) & 3
        left = (tile & 1) * TILE_COLS
        for r in range(TILE_ROWS):
            row = (tile >> 1) * TILE_ROWS + r
            x = ref[r * TILE_COLS : (r + 1) * TILE_COLS, :]
            x = jnp.where((row < meta[0]) & (left + edge < meta[1]), x, jnp.zeros_like(x))
            out[pl.ds(pl.multiple_of(row * COLS + left, TILE_COLS), TILE_COLS), :] = x


def front_kernel(
    meta, xg0, xg1, xg2, xg3, conv, gain, wq, wk, wv,
    xin_o, pre_o, hid_o, nrm_o, q_o, k_o, v_o,
    taps,
):
    third = 3 * CH
    taps[0:COLS, :] = jnp.zeros((COLS, third), bf16)
    taps[CELLS + COLS :, :] = jnp.zeros((COLS, third), bf16)
    col = iota((COLS, 1), 0)

    place_tiles(meta, (xg0, xg1, xg2, xg3), xin_o)
    for r in range(ROWS):
        xb = xin_o[r * COLS : (r + 1) * COLS, :]
        x = xb.astype(f32)
        to = slice((r + 1) * COLS, (r + 2) * COLS)
        taps[to, 0:CH] = jnp.where(col == 0, 0.0, pltpu.roll(x, 1, 0)).astype(bf16)
        taps[to, CH : 2 * CH] = xb
        taps[to, 2 * CH :] = jnp.where(col == COLS - 1, 0.0, pltpu.roll(x, COLS - 1, 0)).astype(bf16)
    for dy in range(3):
        part = dot(taps[dy * COLS : dy * COLS + CELLS, :], conv[dy * third : (dy + 1) * third, :])
        if dy == 0:
            pre_o[...] = part
        else:
            pre_o[...] += part

    step = 64

    def norm(i, carry):
        at = pl.multiple_of(i * step, step)
        rows = pl.ds(at, step)
        pre = pre_o[rows, :]
        act = pre / (1.0 + jnp.exp(-pre))
        hid = jnp.where(valid_rows(meta, at, step), xin_o[rows, :].astype(f32) + act, 0.0)
        hid = hid.astype(bf16)
        hid_o[rows, :] = hid
        hid = hid.astype(f32)
        centred = hid - jnp.mean(hid, axis=1, keepdims=True)
        spread = jnp.mean(centred * centred, axis=1, keepdims=True)
        nrm_o[rows, :] = (centred * lax.rsqrt(spread + EPS) * gain[...]).astype(bf16)
        return carry

    lax.fori_loop(0, CELLS // step, norm, 0)
    nrm = nrm_o[...]
    q_o[...] = (dot(nrm, wq[...]) * (WIDTH**-0.5 * LOG2E)).astype(bf16)
    k_o[...] = dot(nrm, wk[...]).astype(bf16)
    v_o[...] = dot(nrm, wv[...]).astype(bf16)


def back_kernel(
    meta, og0, og1, og2, og3, xin, hid, nrm, pre, q, k, v, gain, wq, wk, wv, wo,
    blk_o, mine_o, theirs_o,
    gb, gc, kt, vt, gt, ctxt, dqt, dk, dv, bias, dn, dpre, wide, padm, padr, gmain, grest, gproj, stage, half,
):
    sy, sx, core = meta[2], meta[3], meta[4]
    col = iota((COLS, 1), 0)

    place_tiles(meta, (og0, og1, og2, og3), gb)
    gc[...] = dot_t(gb[...], wo[...]).astype(bf16)
    kt[...] = k[...].T
    gt[...] = gc[...].T
    for h in range(HEADS):
        vt[h * SLOT : h * SLOT + WIDTH, :] = v[:, h * WIDTH : (h + 1) * WIDTH].T
        vt[h * SLOT + WIDTH : (h + 1) * SLOT, :] = jnp.ones((SLOT - WIDTH, CELLS), bf16)
    lane = iota((1, 2 * WIDTH), 1)
    ok = valid_rows(meta, 0, CELLS)
    for e in range(2):
        bias[e] = jnp.where((lane == WIDTH * (1 - e)) & ~ok, -1e30, 0.0).astype(bf16)

    def stage_a(h):
        lanes = slice(h // 2 * 2 * WIDTH, (h // 2 + 1) * 2 * WIDTH)
        e = h % 2
        own = (lane >= WIDTH * e) & (lane < WIDTH * (e + 1))
        one = jnp.where(lane == WIDTH * (1 - e), 1.0, 0.0).astype(bf16)
        zero = jnp.zeros((), bf16)
        q2, g2 = q[:, lanes], gc[:, lanes]
        s = dot_t(jnp.where(own, k[:, lanes], bias[e]), jnp.where(own, q2, one))
        dp = dot_t(v[:, lanes], jnp.where(own, g2, zero))
        return dict(h=h, s=s, dp=dp, qm=jnp.where(own, q2, zero), gm=jnp.where(own, g2, zero))

    def stage_b(t):
        s = t.pop("s")
        t["ex"] = jnp.exp2(s - jnp.max(s, axis=0, keepdims=True))
        t["eb"] = t["ex"].astype(bf16)

    def stage_c(t):
        h = t["h"]
        rows = slice(h * WIDTH, (h + 1) * WIDTH)
        ctx = dot(vt[h * SLOT : (h + 1) * SLOT, :], t["eb"])
        inv = 1.0 / ctx[WIDTH : WIDTH + 1, :]
        ctx = ctx[:WIDTH, :] * inv
        ctxt[rows, :] = ctx.astype(bf16)
        t["delta"] = jnp.sum(gt[rows, :].astype(f32) * ctx, axis=0, keepdims=True)
        t["inv"] = inv

    def stage_d(t):
        t["ds"] = (t.pop("ex") * (t.pop("dp") - t.pop("delta"))).astype(bf16)

    def stage_e(t):
        h, ds, inv = t["h"], t.pop("ds"), t.pop("inv")
        rows = slice(h * WIDTH, (h + 1) * WIDTH)
        dqt[rows, :] = (dot(kt[rows, :], ds) * (inv * WIDTH**-0.5)).astype(bf16)
        col = jnp.broadcast_to(inv, (8, CELLS)).T[:, 0:1]
        t["dk"] = dot(ds, (t.pop("qm").astype(f32) * col).astype(bf16))
        t["dv"] = dot(t.pop("eb"), (t.pop("gm").astype(f32) * col).astype(bf16))

    def stage_f(t, u):
        lanes = slice(t["h"] * WIDTH, (t["h"] + 2) * WIDTH)
        dk[:, lanes] = ((t["dk"] + u["dk"]) * (1.0 / LOG2E)).astype(bf16)
        dv[:, lanes] = (t["dv"] + u["dv"]).astype(bf16)


    heads = [stage_a(0)]
    for h in range(HEADS + 1):
        if h + 1 < HEADS:
            heads.append(stage_a(h + 1))
        if h < HEADS:
            stage_b(heads[h])
        if h > 0:
            stage_e(heads[h - 1])
        if h < HEADS:
            stage_c(heads[h])
            stage_d(heads[h])
        if h > 0 and h % 2 == 0:
            stage_f(heads[h - 2], heads[h - 1])
    part = CELLS // 2
    at = pl.multiple_of(sy * part, part)
    ctx_half = ctxt[:, pl.ds(at, part)].T
    half[...] = hid[pl.ds(at, part), :].astype(f32) + dot(ctx_half, wo[...])
    for r in range(TILE_ROWS):
        rows = half[pl.ds(pl.multiple_of(r * COLS + sx * TILE_COLS, 16), TILE_COLS), :]
        cells = sx * TILE_COLS + iota((TILE_COLS, 1), 0)
        keep = (sy * TILE_ROWS + r < meta[0]) & (cells < meta[1])
        blk_o[r * TILE_COLS : (r + 1) * TILE_COLS, :] = jnp.where(keep, rows, 0.0).astype(bf16)

    dq = dqt[...].T
    dn[...] = dot_t(dq, wq[...]) + dot_t(dk[...], wk[...]) + dot_t(dv[...], wv[...])
    step = 64

    def norm_back(i, carry):
        at = pl.multiple_of(i * step, step)
        rows = pl.ds(at, step)
        h = hid[rows, :].astype(f32)
        centred = h - jnp.mean(h, axis=1, keepdims=True)
        rstd = lax.rsqrt(jnp.mean(centred * centred, axis=1, keepdims=True) + EPS)
        xhat = centred * rstd
        dx = dn[rows, :] * gain[...]
        m1 = jnp.mean(dx, axis=1, keepdims=True)
        m2 = jnp.mean(dx * xhat, axis=1, keepdims=True)
        dh = gb[rows, :].astype(f32) + rstd * (dx - m1 - xhat * m2)
        a = pre[rows, :]
        sig = 1.0 / (1.0 + jnp.exp(-a))
        out = dh * sig * (1.0 + a * (1.0 - sig))
        dpre[rows, :] = jnp.where(valid_rows(meta, at, step), out, 0.0).astype(bf16)
        return carry

    lax.fori_loop(0, CELLS // step, norm_back, 0)

    first = (sy * 2 + sx) * PART
    row = iota((CH, 1), 0) - first

    def pick(lo, lanes, group=None):
        n = iota((1, lanes), 1)
        want = n + lo if group is None else (n & (REST - 1)) + lo
        hit = row == want
        if group is not None and group >= 0:
            hit = hit & ((n >> 5) == group)
        return jnp.where(hit, 1.0, 0.0).astype(bf16)

    nt = nrm[...].T
    main = pick(0, MAIN)
    grads = (dq, dk[...], dv[...], gb[...])
    mains, rests = [], []
    for w, g in enumerate(grads):
        both = dot(g, jnp.concatenate([main, pick(MAIN, 4 * REST, w)], axis=1))
        mains.append(both[:, :MAIN].astype(bf16))
        rests.append(both[:, MAIN:])
    qkv = dot(nt, jnp.concatenate(mains[:3] + [(rests[0] + rests[1] + rests[2]).astype(bf16)], axis=1))
    out = dot(ctxt[...], jnp.concatenate([mains[3], rests[3].astype(bf16)], axis=1))
    for w in range(3):
        gproj[w * CH : (w + 1) * CH, :] = qkv[:, w * MAIN : (w + 1) * MAIN]
    gproj[3 * CH : 4 * CH, :] = out[:, :MAIN]
    gproj[4 * CH :, :] = qkv[:, 3 * MAIN :] + out[:, MAIN:]

    ccol = iota((CELLS, 1), 0) & (COLS - 1)
    dmain = dot(dpre[...], main)
    drest = dot(dpre[...], pick(MAIN, 3 * MAIN, -1))
    up = lambda x: jnp.where(ccol == COLS - 1, 0.0, pltpu.roll(x, CELLS - 1, 0))
    down = lambda x: jnp.where(ccol == 0, 0.0, pltpu.roll(x, 1, 0))
    padm[...] = jnp.zeros_like(padm)
    padr[...] = jnp.zeros_like(padr)
    inner = slice(COLS, COLS + CELLS)
    padm[0, inner, :] = up(dmain).astype(bf16)
    padm[1, inner, :] = dmain.astype(bf16)
    padm[2, inner, :] = down(dmain).astype(bf16)
    tap = iota((1, 3 * MAIN), 1) >> 5
    tap_dx = tap % 3
    tap_dy = tap // 3
    padr[inner, :] = jnp.where(tap_dx == 0, up(drest), jnp.where(tap_dx == 1, drest, down(drest)))
    for t in range(9):
        lo = (2 - t // 3) * COLS
        wide[:, t * MAIN : (t + 1) * MAIN] = padm[t % 3, lo : lo + CELLS, :]
    wide[:, 9 * MAIN :] = jnp.where(
        tap_dy == 0,
        padr[2 * COLS :, :],
        jnp.where(tap_dy == 1, padr[inner, :], padr[0:CELLS, :]),
    ).astype(bf16)
    xt = xin[...].T
    for j in range(6):
        g = dot(xt, wide[:, j * 256 : (j + 1) * 256])
        for i in range(2):
            t = 2 * j + i
            val = g[:, i * MAIN : (i + 1) * MAIN]
            if t < 9:
                gmain[t * CH : (t + 1) * CH, :] = val
            else:
                for u in range(4):
                    n = (t - 9) * 4 + u
                    if n < 9:
                        grest[n * CH : (n + 1) * CH, 0:REST] = val[:, u * REST : (u + 1) * REST]

    stage[...] = jnp.zeros_like(stage)
    for j in range(PIECES // 2):
        for c in range(2):
            d = 2 * j + c
            for w in range(4):
                stage[c, w * PROJ_ROWS : (w + 1) * PROJ_ROWS, :] = gproj[
                    w * CH + d * PROJ_ROWS : w * CH + (d + 1) * PROJ_ROWS, :
                ]
            stage[c, AT_PROJ_REST : AT_PROJ_REST + PROJ_ROWS, :] = gproj[
                4 * CH + d * PROJ_ROWS : 4 * CH + (d + 1) * PROJ_ROWS, :
            ]
            stage[c, AT_CONV : AT_CONV + CONV_ROWS, :] = gmain[d * CONV_ROWS : (d + 1) * CONV_ROWS, :]
            stage[c, AT_CONV_REST : AT_CONV_REST + QUARTER, :] = jnp.concatenate(
                [
                    grest[d * CONV_ROWS + g * QUARTER : d * CONV_ROWS + (g + 1) * QUARTER, 0:REST]
                    for g in range(4)
                ],
                axis=1,
            )
        zero, one = stage[0], stage[1]
        mine_o[j] = jnp.where(core == 0, zero, one).astype(bf16)
        theirs_o[j] = jnp.where(core == 0, one, zero).astype(bf16)


def last_kernel(pieces, conv_o, q_o, k_o, v_o, o_o, total):
    acc = pieces[0].astype(f32)
    for j in range(1, pieces.shape[0]):
        acc = acc + pieces[j].astype(f32)
    total[...] = acc
    conv_o[:MAIN, :] = total[AT_CONV : AT_CONV + CONV_ROWS, :].T
    rest = jnp.concatenate(
        [
            total[AT_CONV_REST : AT_CONV_REST + QUARTER, g * REST : (g + 1) * REST]
            for g in range(4)
        ],
        axis=0,
    )
    conv_o[MAIN:, :] = rest.T
    for w, out in enumerate((q_o, k_o, v_o, o_o)):
        out[:, :MAIN] = total[w * PROJ_ROWS : (w + 1) * PROJ_ROWS, :]
        out[:, MAIN:] = total[AT_PROJ_REST : AT_PROJ_REST + PROJ_ROWS, w * REST : (w + 1) * REST]


VM = pl.BlockSpec(memory_space=pltpu.VMEM)
SM = pl.BlockSpec(memory_space=pltpu.SMEM)
AN = pl.BlockSpec(memory_space=pl.ANY)


def shape(dims, dtype):
    return jax.ShapeDtypeStruct(dims, dtype)


def front(meta, xg, conv_weight, gain, wq, wk, wv):
    flat = (CELLS, CH)
    return pl.pallas_call(
        front_kernel,
        name="front",
        out_shape=[shape(flat, bf16), shape(flat, f32)] + [shape(flat, bf16)] * 5,
        in_specs=[SM] + [VM] * 9,
        out_specs=[VM] * 7,
        scratch_shapes=[
            pltpu.VMEM((CELLS + 2 * COLS, 3 * CH), bf16),
        ],
        compiler_params=pltpu.CompilerParams(vmem_limit_bytes=24 * 2**20),
    )(meta, *xg, conv_weight, gain, wq, wk, wv)


def back(meta, og, xin, hid, nrm, pre, q, k, v, gain, wq, wk, wv, wo):
    flat, turned = (CELLS, CH), (CH, CELLS)
    return pl.pallas_call(
        back_kernel,
        name="back",
        out_shape=[
            shape((TILE_ROWS * TILE_COLS, CH), bf16),
            shape((PIECES // 2, PIECE, 128), bf16),
            shape((PIECES // 2, PIECE, 128), bf16),
        ],
        in_specs=[SM] + [VM] * 16,
        out_specs=[VM] * 3,
        scratch_shapes=[
            pltpu.VMEM(flat, bf16),
            pltpu.VMEM(flat, bf16),
            pltpu.VMEM(turned, bf16),
            pltpu.VMEM((HEADS * SLOT, CELLS), bf16),
            pltpu.VMEM(turned, bf16),
            pltpu.VMEM(turned, bf16),
            pltpu.VMEM(turned, bf16),
            pltpu.VMEM(flat, bf16),
            pltpu.VMEM(flat, bf16),
            pltpu.VMEM((2, CELLS, 128), bf16),
            pltpu.VMEM(flat, f32),
            pltpu.VMEM(flat, bf16),
            pltpu.VMEM((CELLS, 12 * 128), bf16),
            pltpu.VMEM((3, CELLS + 2 * COLS, 128), bf16),
            pltpu.VMEM((CELLS + 2 * COLS, 3 * 128), f32),
            pltpu.VMEM((9 * CH, 128), f32),
            pltpu.VMEM((9 * CH, 128), f32),
            pltpu.VMEM((5 * CH, 128), f32),
            pltpu.VMEM((2, PIECE, 128), f32),
            pltpu.VMEM((CELLS // 2, CH), f32),
        ],
        compiler_params=pltpu.CompilerParams(vmem_limit_bytes=32 * 2**20),
    )(meta, *og, xin, hid, nrm, pre, q, k, v, gain, wq, wk, wv, wo)


def last(pieces):
    small = shape((PROJ_ROWS, PART), f32)
    return pl.pallas_call(
        last_kernel,
        name="last",
        out_shape=[shape((PART, CONV_ROWS), f32), small, small, small, small],
        in_specs=[VM],
        out_specs=[VM] * 5,
        scratch_shapes=[pltpu.VMEM((PIECE, 128), f32)],
    )(pieces)


def from_ring(own):
    got = [
        lax.ppermute(own, ("sy", "sx"), [(i, (i + shift) % 4) for i in range(4)])
        for shift in (2, 1, 3)
    ]
    return own, got[1], got[0], got[2]


def body(
    features, bucket_ids, bucket_sizes, conv_weight, norm_gain,
    query_weight, key_weight, value_weight, out_weight, out_grad,
):
    chosen = jnp.arange(bucket_sizes.shape[0], dtype=jnp.int32) == bucket_ids[0]
    size = jnp.sum(jnp.where(chosen[:, None], bucket_sizes, 0), axis=0)
    core = lax.axis_index("dp") % 2
    meta = jnp.stack([size[0], size[1], lax.axis_index("sy"), lax.axis_index("sx"), core])
    meta = meta.astype(jnp.int32)
    gain = norm_gain.reshape(1, CH)
    xg = from_ring(features.reshape(-1, CH))
    og = from_ring(out_grad.reshape(-1, CH))
    xin, pre, hid, nrm, q, k, v = front(
        meta, xg, conv_weight, gain, query_weight, key_weight, value_weight
    )
    block, mine, theirs = back(
        meta, og, xin, hid, nrm, pre, q, k, v, gain,
        query_weight, key_weight, value_weight, out_weight,
    )
    count = lax.axis_size("dp")
    other = lax.ppermute(theirs, "dp", [(i, i ^ 1) for i in range(count)])
    both = (mine.astype(f32) + other.astype(f32)).astype(bf16)
    groups = [[c + 2 * i for i in range(count // 2)] for c in range(2)]
    pieces = lax.all_to_all(both, "dp", 0, 0, tiled=True, axis_index_groups=groups)
    conv_t, *grads = last(pieces)
    return (block.reshape(features.shape), conv_t.T, *grads)


def solution(mesh):
    tiles = P("dp", "sy", "sx", None)
    grad = P("dp", ("sy", "sx"))
    return jax.shard_map(
        body,
        mesh=mesh,
        in_specs=(tiles, P("dp"), P(), P(), P(), P(), P(), P(), P(), tiles),
        out_specs=(tiles, grad, grad, grad, grad, grad),
        check_vma=False,
    )
```

```python
import jax
import jax.numpy as jnp
from jax import lax
from jax.experimental import pallas as pl
from jax.experimental.pallas import tpu as pltpu
from jax.sharding import PartitionSpec as P

HEADS = 10
EPS = 1e-05
LOG2E = 1.4426950408889634
SLOT = 64 + 16
ROWS, COLS, CH = 16, 32, 640
CELLS = ROWS * COLS
TILE_ROWS, TILE_COLS = 8, 16
WIDTH = CH // HEADS
PART = CH // 4
MAIN, REST = 128, 32
PIECES = 32
CONV_ROWS = 9 * CH // PIECES
QUARTER = CONV_ROWS // 4
PROJ_ROWS = CH // PIECES
AT_PROJ_REST = 4 * PROJ_ROWS
AT_CONV = 112
AT_CONV_REST = 304
PIECE = 352

f32 = jnp.float32
bf16 = jnp.bfloat16


def dot(a, b):
    return jnp.dot(a, b, preferred_element_type=f32)


def dot_t(a, b):
    return lax.dot_general(a, b, (((1,), (1,)), ((), ())), preferred_element_type=f32)


def iota(shape, dim):
    return lax.broadcasted_iota(jnp.int32, shape, dim)


def valid_rows(meta, start, count):
    cell = start + iota((count, 1), 0)
    return ((cell >> 5) < meta[0]) & ((cell & 31) < meta[1])


def place_tiles(meta, tiles, out):
    edge = iota((TILE_COLS, 1), 0)
    for shift, ref in enumerate(tiles):
        tile = (meta[2] * 2 + meta[3] - shift) & 3
        left = (tile & 1) * TILE_COLS
        for r in range(TILE_ROWS):
            row = (tile >> 1) * TILE_ROWS + r
            x = ref[r * TILE_COLS : (r + 1) * TILE_COLS, :]
            x = jnp.where((row < meta[0]) & (left + edge < meta[1]), x, jnp.zeros_like(x))
            out[pl.ds(pl.multiple_of(row * COLS + left, TILE_COLS), TILE_COLS), :] = x


def front_kernel(
    meta, xg0, xg1, xg2, xg3, conv_hbm, gain, wq, wk, wv,
    xin_o, pre_o, hid_o, nrm_o, q_o, k_o, v_o,
    taps, conv, sems,
):
    third = 3 * CH
    copies = [
        pltpu.make_async_copy(
            conv_hbm.at[pl.ds(i * third, third)], conv.at[pl.ds(i * third, third)], sems.at[i]
        )
        for i in range(3)
    ]
    for copy in copies:
        copy.start()
    taps[0:COLS, :] = jnp.zeros((COLS, third), bf16)
    taps[CELLS + COLS :, :] = jnp.zeros((COLS, third), bf16)
    col = iota((COLS, 1), 0)

    place_tiles(meta, (xg0, xg1, xg2, xg3), xin_o)
    for r in range(ROWS):
        xb = xin_o[r * COLS : (r + 1) * COLS, :]
        x = xb.astype(f32)
        to = slice((r + 1) * COLS, (r + 2) * COLS)
        taps[to, 0:CH] = jnp.where(col == 0, 0.0, pltpu.roll(x, 1, 0)).astype(bf16)
        taps[to, CH : 2 * CH] = xb
        taps[to, 2 * CH :] = jnp.where(col == COLS - 1, 0.0, pltpu.roll(x, COLS - 1, 0)).astype(bf16)
    for dy in range(3):
        copies[dy].wait()
        part = dot(taps[dy * COLS : dy * COLS + CELLS, :], conv[dy * third : (dy + 1) * third, :])
        if dy == 0:
            pre_o[...] = part
        else:
            pre_o[...] += part

    step = 64

    def norm(i, carry):
        at = pl.multiple_of(i * step, step)
        rows = pl.ds(at, step)
        pre = pre_o[rows, :]
        act = pre / (1.0 + jnp.exp(-pre))
        hid = jnp.where(valid_rows(meta, at, step), xin_o[rows, :].astype(f32) + act, 0.0)
        hid = hid.astype(bf16)
        hid_o[rows, :] = hid
        hid = hid.astype(f32)
        centred = hid - jnp.mean(hid, axis=1, keepdims=True)
        spread = jnp.mean(centred * centred, axis=1, keepdims=True)
        nrm_o[rows, :] = (centred * lax.rsqrt(spread + EPS) * gain[...]).astype(bf16)
        return carry

    lax.fori_loop(0, CELLS // step, norm, 0, unroll=True)
    nrm = nrm_o[...]
    q_o[...] = (dot(nrm, wq[...]) * (WIDTH**-0.5 * LOG2E)).astype(bf16)
    k_o[...] = dot(nrm, wk[...]).astype(bf16)
    v_o[...] = dot(nrm, wv[...]).astype(bf16)


def back_kernel(
    meta, og0, og1, og2, og3, xin, hid, nrm, pre, q, k, v, gain, wq, wk, wv, wo,
    theirs_o, ctx_o, gproj, gmain, grest,
    gb, gc, kt, vt, gt, ctxt, dqt, dk, dv, bias, dn, dpre, wide, padm, padr, stage,
):
    sy, sx = meta[2], meta[3]
    col = iota((COLS, 1), 0)

    place_tiles(meta, (og0, og1, og2, og3), gb)
    gc[...] = dot_t(gb[...], wo[...]).astype(bf16)
    kt[...] = k[...].T
    gt[...] = gc[...].T
    for h in range(HEADS):
        vt[h * SLOT : h * SLOT + WIDTH, :] = v[:, h * WIDTH : (h + 1) * WIDTH].T
        vt[h * SLOT + WIDTH : (h + 1) * SLOT, :] = jnp.ones((SLOT - WIDTH, CELLS), bf16)
    lane = iota((1, 2 * WIDTH), 1)
    ok = valid_rows(meta, 0, CELLS)
    for e in range(2):
        bias[e] = jnp.where((lane == WIDTH * (1 - e)) & ~ok, -1e30, 0.0).astype(bf16)

    def stage_a(h):
        lanes = slice(h // 2 * 2 * WIDTH, (h // 2 + 1) * 2 * WIDTH)
        e = h % 2
        own = (lane >= WIDTH * e) & (lane < WIDTH * (e + 1))
        one = jnp.where(lane == WIDTH * (1 - e), 1.0, 0.0).astype(bf16)
        zero = jnp.zeros((), bf16)
        q2, g2 = q[:, lanes], gc[:, lanes]
        s = dot_t(jnp.where(own, k[:, lanes], bias[e]), jnp.where(own, q2, one))
        dp = dot_t(v[:, lanes], jnp.where(own, g2, zero))
        return dict(h=h, s=s, dp=dp, qm=jnp.where(own, q2, zero), gm=jnp.where(own, g2, zero))

    def stage_b(t):
        s = t.pop("s")
        t["ex"] = jnp.exp2(s - jnp.max(s, axis=0, keepdims=True))
        t["eb"] = t["ex"].astype(bf16)

    def stage_c(t):
        h = t["h"]
        rows = slice(h * WIDTH, (h + 1) * WIDTH)
        ctx = dot(vt[h * SLOT : (h + 1) * SLOT, :], t["eb"])
        inv = 1.0 / ctx[WIDTH : WIDTH + 1, :]
        ctx = ctx[:WIDTH, :] * inv
        ctxt[rows, :] = ctx.astype(bf16)
        t["delta"] = jnp.sum(gt[rows, :].astype(f32) * ctx, axis=0, keepdims=True)
        t["inv"] = inv

    def stage_d(t):
        t["ds"] = (t.pop("ex") * (t.pop("dp") - t.pop("delta"))).astype(bf16)

    def stage_e(t):
        h, ds, inv = t["h"], t.pop("ds"), t.pop("inv")
        rows = slice(h * WIDTH, (h + 1) * WIDTH)
        dqt[rows, :] = (dot(kt[rows, :], ds) * (inv * WIDTH**-0.5)).astype(bf16)
        col = jnp.broadcast_to(inv, (8, CELLS)).T[:, 0:1]
        t["dk"] = dot(ds, (t.pop("qm").astype(f32) * col).astype(bf16))
        t["dv"] = dot(t.pop("eb"), (t.pop("gm").astype(f32) * col).astype(bf16))

    def stage_f(t, u):
        lanes = slice(t["h"] * WIDTH, (t["h"] + 2) * WIDTH)
        dk[:, lanes] = ((t["dk"] + u["dk"]) * (1.0 / LOG2E)).astype(bf16)
        dv[:, lanes] = (t["dv"] + u["dv"]).astype(bf16)


    heads = [stage_a(0)]
    for h in range(HEADS + 1):
        if h + 1 < HEADS:
            heads.append(stage_a(h + 1))
        if h < HEADS:
            stage_b(heads[h])
        if h > 0:
            stage_e(heads[h - 1])
        if h < HEADS:
            stage_c(heads[h])
            stage_d(heads[h])
        if h > 0 and h % 2 == 0:
            stage_f(heads[h - 2], heads[h - 1])
    ctx_o[...] = ctxt[:, pl.ds(pl.multiple_of(sy * (CELLS // 2), CELLS // 2), CELLS // 2)].T
    dq = dqt[...].T
    dn[...] = dot_t(dq, wq[...]) + dot_t(dk[...], wk[...]) + dot_t(dv[...], wv[...])
    step = 64

    def norm_back(i, carry):
        at = pl.multiple_of(i * step, step)
        rows = pl.ds(at, step)
        h = hid[rows, :].astype(f32)
        centred = h - jnp.mean(h, axis=1, keepdims=True)
        rstd = lax.rsqrt(jnp.mean(centred * centred, axis=1, keepdims=True) + EPS)
        xhat = centred * rstd
        dx = dn[rows, :] * gain[...]
        m1 = jnp.mean(dx, axis=1, keepdims=True)
        m2 = jnp.mean(dx * xhat, axis=1, keepdims=True)
        dh = gb[rows, :].astype(f32) + rstd * (dx - m1 - xhat * m2)
        a = pre[rows, :]
        sig = 1.0 / (1.0 + jnp.exp(-a))
        out = dh * sig * (1.0 + a * (1.0 - sig))
        dpre[rows, :] = jnp.where(valid_rows(meta, at, step), out, 0.0).astype(bf16)
        return carry

    lax.fori_loop(0, CELLS // step, norm_back, 0, unroll=True)

    first = (sy * 2 + sx) * PART
    row = iota((CH, 1), 0) - first

    def pick(lo, lanes, group=None):
        n = iota((1, lanes), 1)
        want = n + lo if group is None else (n & (REST - 1)) + lo
        hit = row == want
        if group is not None and group >= 0:
            hit = hit & ((n >> 5) == group)
        return jnp.where(hit, 1.0, 0.0).astype(bf16)

    nt = nrm[...].T
    main = pick(0, MAIN)
    grads = (dq, dk[...], dv[...], gb[...])
    mains, rests = [], []
    for w, g in enumerate(grads):
        both = dot(g, jnp.concatenate([main, pick(MAIN, 4 * REST, w)], axis=1))
        mains.append(both[:, :MAIN].astype(bf16))
        rests.append(both[:, MAIN:])
    qkv = dot(nt, jnp.concatenate(mains[:3] + [(rests[0] + rests[1] + rests[2]).astype(bf16)], axis=1))
    out = dot(ctxt[...], jnp.concatenate([mains[3], rests[3].astype(bf16)], axis=1))
    for w in range(3):
        gproj[w * CH : (w + 1) * CH, :] = qkv[:, w * MAIN : (w + 1) * MAIN]
    gproj[3 * CH : 4 * CH, :] = out[:, :MAIN]
    gproj[4 * CH :, :] = qkv[:, 3 * MAIN :] + out[:, MAIN:]

    ccol = iota((CELLS, 1), 0) & (COLS - 1)
    dmain = dot(dpre[...], main)
    drest = dot(dpre[...], pick(MAIN, 3 * MAIN, -1))
    up = lambda x: jnp.where(ccol == COLS - 1, 0.0, pltpu.roll(x, CELLS - 1, 0))
    down = lambda x: jnp.where(ccol == 0, 0.0, pltpu.roll(x, 1, 0))
    padm[...] = jnp.zeros_like(padm)
    padr[...] = jnp.zeros_like(padr)
    inner = slice(COLS, COLS + CELLS)
    padm[0, inner, :] = up(dmain).astype(bf16)
    padm[1, inner, :] = dmain.astype(bf16)
    padm[2, inner, :] = down(dmain).astype(bf16)
    tap = iota((1, 3 * MAIN), 1) >> 5
    tap_dx = tap % 3
    tap_dy = tap // 3
    padr[inner, :] = jnp.where(tap_dx == 0, up(drest), jnp.where(tap_dx == 1, drest, down(drest)))
    for t in range(9):
        lo = (2 - t // 3) * COLS
        wide[:, t * MAIN : (t + 1) * MAIN] = padm[t % 3, lo : lo + CELLS, :]
    wide[:, 9 * MAIN :] = jnp.where(
        tap_dy == 0,
        padr[2 * COLS :, :],
        jnp.where(tap_dy == 1, padr[inner, :], padr[0:CELLS, :]),
    ).astype(bf16)
    xt = xin[...].T
    for j in range(6):
        g = dot(xt, wide[:, j * 256 : (j + 1) * 256])
        for i in range(2):
            t = 2 * j + i
            val = g[:, i * MAIN : (i + 1) * MAIN]
            if t < 9:
                gmain[t * CH : (t + 1) * CH, :] = val
            else:
                for u in range(4):
                    n = (t - 9) * 4 + u
                    if n < 9:
                        grest[n * CH : (n + 1) * CH, 0:REST] = val[:, u * REST : (u + 1) * REST]

    pack(meta, 1, gproj, gmain, grest, stage, theirs_o)


def pack(meta, flip, gproj, gmain, grest, stage, out):
    stage[...] = jnp.zeros_like(stage)
    for j in range(PIECES // 2):
        for c in range(2):
            d = 2 * j + c
            for w in range(5):
                stage[c, w * PROJ_ROWS : (w + 1) * PROJ_ROWS, :] = gproj[
                    w * CH + d * PROJ_ROWS : w * CH + (d + 1) * PROJ_ROWS, :
                ]
            stage[c, AT_CONV : AT_CONV + CONV_ROWS, :] = gmain[d * CONV_ROWS : (d + 1) * CONV_ROWS, :]
            stage[c, AT_CONV_REST : AT_CONV_REST + QUARTER, :] = jnp.concatenate(
                [
                    grest[d * CONV_ROWS + g * QUARTER : d * CONV_ROWS + (g + 1) * QUARTER, 0:REST]
                    for g in range(4)
                ],
                axis=1,
            )
        out[j] = jnp.where(meta[4] == flip, stage[0], stage[1]).astype(bf16)


def rest_kernel(meta, ctx, hid, wo, gproj, gmain, grest, blk_o, mine_o, stage, half):
    sy, sx = meta[2], meta[3]
    part = CELLS // 2
    at = pl.multiple_of(sy * part, part)
    half[...] = hid[pl.ds(at, part), :].astype(f32) + dot(ctx[...], wo[...])
    for r in range(TILE_ROWS):
        rows = half[pl.ds(pl.multiple_of(r * COLS + sx * TILE_COLS, 16), TILE_COLS), :]
        cells = sx * TILE_COLS + iota((TILE_COLS, 1), 0)
        keep = (sy * TILE_ROWS + r < meta[0]) & (cells < meta[1])
        blk_o[r * TILE_COLS : (r + 1) * TILE_COLS, :] = jnp.where(keep, rows, 0.0).astype(bf16)
    pack(meta, 0, gproj, gmain, grest, stage, mine_o)


def last_kernel(pieces, conv_o, q_o, k_o, v_o, o_o, total):
    acc = pieces[0].astype(f32)
    for j in range(1, pieces.shape[0]):
        acc = acc + pieces[j].astype(f32)
    total[...] = acc
    conv_o[:MAIN, :] = total[AT_CONV : AT_CONV + CONV_ROWS, :].T
    rest = jnp.concatenate(
        [
            total[AT_CONV_REST : AT_CONV_REST + QUARTER, g * REST : (g + 1) * REST]
            for g in range(4)
        ],
        axis=0,
    )
    conv_o[MAIN:, :] = rest.T
    for w, out in enumerate((q_o, k_o, v_o, o_o)):
        out[:, :MAIN] = total[w * PROJ_ROWS : (w + 1) * PROJ_ROWS, :]
        out[:, MAIN:] = total[AT_PROJ_REST : AT_PROJ_REST + PROJ_ROWS, w * REST : (w + 1) * REST]


VM = pl.BlockSpec(memory_space=pltpu.VMEM)
SM = pl.BlockSpec(memory_space=pltpu.SMEM)
HB = pl.BlockSpec(memory_space=pltpu.HBM)


def shape(dims, dtype):
    return jax.ShapeDtypeStruct(dims, dtype)


def fetch_kernel(*refs):
    count = (len(refs) - 1) // 2
    copies = [
        pltpu.make_async_copy(refs[i], refs[count + i], refs[-1].at[i]) for i in range(count)
    ]
    for copy in copies:
        copy.start()
    for copy in copies:
        copy.wait()


def fetch(*arrays):
    return pl.pallas_call(
        fetch_kernel,
        name="fetch",
        out_shape=[shape(a.shape, a.dtype) for a in arrays],
        in_specs=[HB] * len(arrays),
        out_specs=[VM] * len(arrays),
        scratch_shapes=[pltpu.SemaphoreType.DMA((len(arrays),))],
        compiler_params=pltpu.CompilerParams(vmem_limit_bytes=16 * 2**20),
    )(*arrays)


def front(meta, xg, conv_weight, gain, wq, wk, wv):
    flat = (CELLS, CH)
    return pl.pallas_call(
        front_kernel,
        name="front",
        out_shape=[shape(flat, bf16), shape(flat, f32)] + [shape(flat, bf16)] * 5,
        in_specs=[SM] + [VM] * 4 + [HB] + [VM] * 4,
        out_specs=[VM] * 7,
        scratch_shapes=[
            pltpu.VMEM((CELLS + 2 * COLS, 3 * CH), bf16),
            pltpu.VMEM((9 * CH, CH), bf16),
            pltpu.SemaphoreType.DMA((3,)),
        ],
        compiler_params=pltpu.CompilerParams(vmem_limit_bytes=42 * 2**20),
    )(meta, *xg, conv_weight, gain, wq, wk, wv)


def back(meta, og, xin, hid, nrm, pre, q, k, v, gain, wq, wk, wv, wo):
    flat, turned = (CELLS, CH), (CH, CELLS)
    return pl.pallas_call(
        back_kernel,
        name="back",
        out_shape=[
            shape((PIECES // 2, PIECE, 128), bf16),
            shape((CELLS // 2, CH), bf16),
            shape((5 * CH, 128), f32),
            shape((9 * CH, 128), f32),
            shape((9 * CH, 128), f32),
        ],
        in_specs=[SM] + [VM] * 16,
        out_specs=[VM] * 5,
        scratch_shapes=[
            pltpu.VMEM(flat, bf16),
            pltpu.VMEM(flat, bf16),
            pltpu.VMEM(turned, bf16),
            pltpu.VMEM((HEADS * SLOT, CELLS), bf16),
            pltpu.VMEM(turned, bf16),
            pltpu.VMEM(turned, bf16),
            pltpu.VMEM(turned, bf16),
            pltpu.VMEM(flat, bf16),
            pltpu.VMEM(flat, bf16),
            pltpu.VMEM((2, CELLS, 128), bf16),
            pltpu.VMEM(flat, f32),
            pltpu.VMEM(flat, bf16),
            pltpu.VMEM((CELLS, 12 * 128), bf16),
            pltpu.VMEM((3, CELLS + 2 * COLS, 128), bf16),
            pltpu.VMEM((CELLS + 2 * COLS, 3 * 128), f32),
            pltpu.VMEM((2, PIECE, 128), f32),
        ],
        compiler_params=pltpu.CompilerParams(vmem_limit_bytes=32 * 2**20),
    )(meta, *og, xin, hid, nrm, pre, q, k, v, gain, wq, wk, wv, wo)


def rest(meta, ctx, hid, wo, gproj, gmain, grest):
    return pl.pallas_call(
        rest_kernel,
        name="rest",
        out_shape=[
            shape((TILE_ROWS * TILE_COLS, CH), bf16),
            shape((PIECES // 2, PIECE, 128), bf16),
        ],
        in_specs=[SM] + [VM] * 6,
        out_specs=[VM] * 2,
        scratch_shapes=[
            pltpu.VMEM((2, PIECE, 128), f32),
            pltpu.VMEM((CELLS // 2, CH), f32),
        ],
        compiler_params=pltpu.CompilerParams(vmem_limit_bytes=20 * 2**20),
    )(meta, ctx, hid, wo, gproj, gmain, grest)


def last(pieces):
    small = shape((PROJ_ROWS, PART), f32)
    return pl.pallas_call(
        last_kernel,
        name="last",
        out_shape=[shape((PART, CONV_ROWS), f32), small, small, small, small],
        in_specs=[VM],
        out_specs=[VM] * 5,
        scratch_shapes=[pltpu.VMEM((PIECE, 128), f32)],
    )(pieces)


def from_ring(own, turn):
    ring = ("sy", "sx")
    ahead = lax.ppermute(own, ring, [(i, (i + 3) % 4) for i in range(4)])
    if turn:
        across = lax.ppermute(ahead, ring, [(i, (i + 3) % 4) for i in range(4)])
    else:
        across = lax.ppermute(own, ring, [(i, (i + 2) % 4) for i in range(4)])
    behind = lax.ppermute(own, ring, [(i, (i + 1) % 4) for i in range(4)])
    return behind, across, ahead


def body(
    features, bucket_ids, bucket_sizes, conv_weight, norm_gain,
    query_weight, key_weight, value_weight, out_weight, out_grad,
):
    chosen = jnp.arange(bucket_sizes.shape[0], dtype=jnp.int32) == bucket_ids[0]
    size = jnp.sum(jnp.where(chosen[:, None], bucket_sizes, 0), axis=0)
    core = lax.axis_index("dp") % 2
    meta = jnp.stack([size[0], size[1], lax.axis_index("sy"), lax.axis_index("sx"), core])
    meta = meta.astype(jnp.int32)
    gain = norm_gain.reshape(1, CH)
    x, g = features.reshape(-1, CH), out_grad.reshape(-1, CH)
    query_weight, key_weight, value_weight, out_weight, x_near, g_near = fetch(
        query_weight, key_weight, value_weight, out_weight, x, g
    )
    xg = (x_near, *from_ring(x, False))
    og = (g_near, *from_ring(g, True))
    xin, pre, hid, nrm, q, k, v = front(
        meta, xg, conv_weight, gain, query_weight, key_weight, value_weight
    )
    theirs, ctx, *grads = back(
        meta, og, xin, hid, nrm, pre, q, k, v, gain,
        query_weight, key_weight, value_weight, out_weight,
    )
    count = lax.axis_size("dp")
    other = lax.ppermute(theirs, "dp", [(i, i ^ 1) for i in range(count)])
    block, mine = rest(meta, ctx, hid, out_weight, *grads)
    both = (mine.astype(f32) + other.astype(f32)).astype(bf16)
    groups = [[c + 2 * i for i in range(count // 2)] for c in range(2)]
    pieces = lax.all_to_all(both, "dp", 0, 0, tiled=True, axis_index_groups=groups)
    conv_t, *grads = last(pieces)
    return (block.reshape(features.shape), conv_t.T, *grads)


def solution(mesh):
    tiles = P("dp", "sy", "sx", None)
    grad = P("dp", ("sy", "sx"))
    return jax.shard_map(
        body,
        mesh=mesh,
        in_specs=(tiles, P("dp"), P(), P(), P(), P(), P(), P(), P(), tiles),
        out_specs=(tiles, grad, grad, grad, grad, grad),
        check_vma=False,
    )
```

```python
import jax
import jax.numpy as jnp
from jax import lax
from jax.experimental import pallas as pl
from jax.experimental.pallas import tpu as pltpu
from jax.sharding import PartitionSpec as P

HEADS = 10
EPS = 1e-05
LOG2E = 1.4426950408889634
SLOT = 64 + 16
ROWS, COLS, CH = 16, 32, 640
CELLS = ROWS * COLS
TILE_ROWS, TILE_COLS = 8, 16
WIDTH = CH // HEADS
PART = CH // 4
MAIN, REST = 128, 32
PIECES = 32
CONV_ROWS = 9 * CH // PIECES
QUARTER = CONV_ROWS // 4
PROJ_ROWS = CH // PIECES
AT_PROJ_REST = 4 * PROJ_ROWS
AT_CONV = 112
AT_CONV_REST = 304
PIECE = 352

f32 = jnp.float32
bf16 = jnp.bfloat16


def dot(a, b):
    return jnp.dot(a, b, preferred_element_type=f32)


def dot_t(a, b):
    return lax.dot_general(a, b, (((1,), (1,)), ((), ())), preferred_element_type=f32)


def iota(shape, dim):
    return lax.broadcasted_iota(jnp.int32, shape, dim)


def place_of(bucket, sizes):
    core = lax.axis_index("dp") & 1
    b = bucket[0]
    return sizes[b, 0], sizes[b, 1], lax.axis_index("sy"), lax.axis_index("sx"), core


def valid_rows(meta, start, count):
    cell = start + iota((count, 1), 0)
    return ((cell >> 5) < meta[0]) & ((cell & 31) < meta[1])


def place_tiles(meta, tiles, out):
    edge = iota((TILE_COLS, 1), 0)
    for shift, ref in enumerate(tiles):
        tile = (meta[2] * 2 + meta[3] - shift) & 3
        left = (tile & 1) * TILE_COLS
        for r in range(TILE_ROWS):
            row = (tile >> 1) * TILE_ROWS + r
            x = ref[r * TILE_COLS : (r + 1) * TILE_COLS, :]
            x = jnp.where((row < meta[0]) & (left + edge < meta[1]), x, jnp.zeros_like(x))
            out[pl.ds(pl.multiple_of(row * COLS + left, TILE_COLS), TILE_COLS), :] = x


def front_kernel(
    bucket, sizes, xg0, xg1, xg2, xg3, conv_hbm, gain,
    xin_o, pre_o, hid_o, nrm_o,
    taps, conv, sems,
):
    meta = place_of(bucket, sizes)
    third = 3 * CH
    copies = [
        pltpu.make_async_copy(
            conv_hbm.at[pl.ds(i * third, third)], conv.at[pl.ds(i * third, third)], sems.at[i]
        )
        for i in range(3)
    ]
    for copy in copies:
        copy.start()
    taps[0:COLS, :] = jnp.zeros((COLS, third), bf16)
    taps[CELLS + COLS :, :] = jnp.zeros((COLS, third), bf16)
    col = iota((COLS, 1), 0)

    place_tiles(meta, (xg0, xg1, xg2, xg3), xin_o)
    for r in range(ROWS):
        xb = xin_o[r * COLS : (r + 1) * COLS, :]
        x = xb.astype(f32)
        to = slice((r + 1) * COLS, (r + 2) * COLS)
        taps[to, 0:CH] = jnp.where(col == 0, 0.0, pltpu.roll(x, 1, 0)).astype(bf16)
        taps[to, CH : 2 * CH] = xb
        taps[to, 2 * CH :] = jnp.where(col == COLS - 1, 0.0, pltpu.roll(x, COLS - 1, 0)).astype(bf16)
    for dy in range(3):
        copies[dy].wait()
        part = dot(taps[dy * COLS : dy * COLS + CELLS, :], conv[dy * third : (dy + 1) * third, :])
        if dy == 0:
            pre_o[...] = part
        else:
            pre_o[...] += part

    step = 64

    def norm(i, carry):
        at = pl.multiple_of(i * step, step)
        rows = pl.ds(at, step)
        pre = pre_o[rows, :]
        act = pre / (1.0 + jnp.exp(-pre))
        hid = jnp.where(valid_rows(meta, at, step), xin_o[rows, :].astype(f32) + act, 0.0)
        hid = hid.astype(bf16)
        hid_o[rows, :] = hid
        hid = hid.astype(f32)
        centred = hid - jnp.mean(hid, axis=1, keepdims=True)
        spread = jnp.mean(centred * centred, axis=1, keepdims=True)
        nrm_o[rows, :] = (centred * lax.rsqrt(spread + EPS) * gain[...]).astype(bf16)
        return carry

    lax.fori_loop(0, CELLS // step, norm, 0, unroll=True)


def back_kernel(
    bucket, sizes, og0, og1, og2, og3, xin, hid, nrm, pre, gain, wq, wk, wv, wo,
    theirs_o, ctx_o, gproj, gmain, grest,
    q, k, v, gb, gc, kt, vt, gt, ctxt, dqt, dk, dv, bias, dn, dpre, wide, padm, padr, stage,
):
    meta = place_of(bucket, sizes)
    sy, sx = meta[2], meta[3]
    col = iota((COLS, 1), 0)

    place_tiles(meta, (og0, og1, og2, og3), gb)
    normed = nrm[...]
    q[...] = (dot(normed, wq[...]) * (WIDTH**-0.5 * LOG2E)).astype(bf16)
    k[...] = dot(normed, wk[...]).astype(bf16)
    v[...] = dot(normed, wv[...]).astype(bf16)
    gc[...] = dot_t(gb[...], wo[...]).astype(bf16)
    kt[...] = k[...].T
    gt[...] = gc[...].T
    for h in range(HEADS):
        vt[h * SLOT : h * SLOT + WIDTH, :] = v[:, h * WIDTH : (h + 1) * WIDTH].T
        vt[h * SLOT + WIDTH : (h + 1) * SLOT, :] = jnp.ones((SLOT - WIDTH, CELLS), bf16)
    lane = iota((1, 2 * WIDTH), 1)
    ok = valid_rows(meta, 0, CELLS)
    for e in range(2):
        bias[e] = jnp.where((lane == WIDTH * (1 - e)) & ~ok, -1e30, 0.0).astype(bf16)

    def stage_a(h):
        lanes = slice(h // 2 * 2 * WIDTH, (h // 2 + 1) * 2 * WIDTH)
        e = h % 2
        own = (lane >= WIDTH * e) & (lane < WIDTH * (e + 1))
        one = jnp.where(lane == WIDTH * (1 - e), 1.0, 0.0).astype(bf16)
        zero = jnp.zeros((), bf16)
        q2, g2 = q[:, lanes], gc[:, lanes]
        s = dot_t(jnp.where(own, k[:, lanes], bias[e]), jnp.where(own, q2, one))
        dp = dot_t(v[:, lanes], jnp.where(own, g2, zero))
        return dict(h=h, s=s, dp=dp, qm=jnp.where(own, q2, zero), gm=jnp.where(own, g2, zero))

    def stage_b(t):
        s = t.pop("s")
        t["ex"] = jnp.exp2(s - jnp.max(s, axis=0, keepdims=True))
        t["eb"] = t["ex"].astype(bf16)

    def stage_c(t):
        h = t["h"]
        rows = slice(h * WIDTH, (h + 1) * WIDTH)
        ctx = dot(vt[h * SLOT : (h + 1) * SLOT, :], t["eb"])
        inv = 1.0 / ctx[WIDTH : WIDTH + 1, :]
        ctx = ctx[:WIDTH, :] * inv
        ctxt[rows, :] = ctx.astype(bf16)
        t["delta"] = jnp.sum(gt[rows, :].astype(f32) * ctx, axis=0, keepdims=True)
        t["inv"] = inv

    def stage_d(t):
        t["ds"] = (t.pop("ex") * (t.pop("dp") - t.pop("delta"))).astype(bf16)

    def stage_e(t):
        h, ds, inv = t["h"], t.pop("ds"), t.pop("inv")
        rows = slice(h * WIDTH, (h + 1) * WIDTH)
        dqt[rows, :] = (dot(kt[rows, :], ds) * (inv * WIDTH**-0.5)).astype(bf16)
        col = jnp.broadcast_to(inv, (8, CELLS)).T[:, 0:1]
        t["dk"] = dot(ds, (t.pop("qm").astype(f32) * col).astype(bf16))
        t["dv"] = dot(t.pop("eb"), (t.pop("gm").astype(f32) * col).astype(bf16))

    def stage_f(t, u):
        lanes = slice(t["h"] * WIDTH, (t["h"] + 2) * WIDTH)
        dk[:, lanes] = ((t["dk"] + u["dk"]) * (1.0 / LOG2E)).astype(bf16)
        dv[:, lanes] = (t["dv"] + u["dv"]).astype(bf16)


    heads = [stage_a(0)]
    for h in range(HEADS + 1):
        if h + 1 < HEADS:
            heads.append(stage_a(h + 1))
        if h < HEADS:
            stage_b(heads[h])
        if h > 0:
            stage_e(heads[h - 1])
        if h < HEADS:
            stage_c(heads[h])
            stage_d(heads[h])
        if h > 0 and h % 2 == 0:
            stage_f(heads[h - 2], heads[h - 1])
    ctx_o[...] = ctxt[:, pl.ds(pl.multiple_of(sy * (CELLS // 2), CELLS // 2), CELLS // 2)].T
    dq = dqt[...].T
    dn[...] = dot_t(dq, wq[...]) + dot_t(dk[...], wk[...]) + dot_t(dv[...], wv[...])
    step = 64

    def norm_back(i, carry):
        at = pl.multiple_of(i * step, step)
        rows = pl.ds(at, step)
        h = hid[rows, :].astype(f32)
        centred = h - jnp.mean(h, axis=1, keepdims=True)
        rstd = lax.rsqrt(jnp.mean(centred * centred, axis=1, keepdims=True) + EPS)
        xhat = centred * rstd
        dx = dn[rows, :] * gain[...]
        m1 = jnp.mean(dx, axis=1, keepdims=True)
        m2 = jnp.mean(dx * xhat, axis=1, keepdims=True)
        dh = gb[rows, :].astype(f32) + rstd * (dx - m1 - xhat * m2)
        a = pre[rows, :]
        sig = 1.0 / (1.0 + jnp.exp(-a))
        out = dh * sig * (1.0 + a * (1.0 - sig))
        dpre[rows, :] = jnp.where(valid_rows(meta, at, step), out, 0.0).astype(bf16)
        return carry

    lax.fori_loop(0, CELLS // step, norm_back, 0, unroll=True)

    first = (sy * 2 + sx) * PART
    row = iota((CH, 1), 0) - first

    def pick(lo, lanes, group=None):
        n = iota((1, lanes), 1)
        want = n + lo if group is None else (n & (REST - 1)) + lo
        hit = row == want
        if group is not None and group >= 0:
            hit = hit & ((n >> 5) == group)
        return jnp.where(hit, 1.0, 0.0).astype(bf16)

    nt = nrm[...].T
    main = pick(0, MAIN)
    grads = (dq, dk[...], dv[...], gb[...])
    mains, rests = [], []
    for w, g in enumerate(grads):
        both = dot(g, jnp.concatenate([main, pick(MAIN, 4 * REST, w)], axis=1))
        mains.append(both[:, :MAIN].astype(bf16))
        rests.append(both[:, MAIN:])
    qkv = dot(nt, jnp.concatenate(mains[:3] + [(rests[0] + rests[1] + rests[2]).astype(bf16)], axis=1))
    out = dot(ctxt[...], jnp.concatenate([mains[3], rests[3].astype(bf16)], axis=1))
    for w in range(3):
        gproj[w * CH : (w + 1) * CH, :] = qkv[:, w * MAIN : (w + 1) * MAIN]
    gproj[3 * CH : 4 * CH, :] = out[:, :MAIN]
    gproj[4 * CH :, :] = qkv[:, 3 * MAIN :] + out[:, MAIN:]

    ccol = iota((CELLS, 1), 0) & (COLS - 1)
    dmain = dot(dpre[...], main)
    drest = dot(dpre[...], pick(MAIN, 3 * MAIN, -1))
    up = lambda x: jnp.where(ccol == COLS - 1, 0.0, pltpu.roll(x, CELLS - 1, 0))
    down = lambda x: jnp.where(ccol == 0, 0.0, pltpu.roll(x, 1, 0))
    padm[...] = jnp.zeros_like(padm)
    padr[...] = jnp.zeros_like(padr)
    inner = slice(COLS, COLS + CELLS)
    padm[0, inner, :] = up(dmain).astype(bf16)
    padm[1, inner, :] = dmain.astype(bf16)
    padm[2, inner, :] = down(dmain).astype(bf16)
    tap = iota((1, 3 * MAIN), 1) >> 5
    tap_dx = tap % 3
    tap_dy = tap // 3
    padr[inner, :] = jnp.where(tap_dx == 0, up(drest), jnp.where(tap_dx == 1, drest, down(drest)))
    for t in range(9):
        lo = (2 - t // 3) * COLS
        wide[:, t * MAIN : (t + 1) * MAIN] = padm[t % 3, lo : lo + CELLS, :]
    wide[:, 9 * MAIN :] = jnp.where(
        tap_dy == 0,
        padr[2 * COLS :, :],
        jnp.where(tap_dy == 1, padr[inner, :], padr[0:CELLS, :]),
    ).astype(bf16)
    xt = xin[...].T
    for j in range(6):
        g = dot(xt, wide[:, j * 256 : (j + 1) * 256])
        for i in range(2):
            t = 2 * j + i
            val = g[:, i * MAIN : (i + 1) * MAIN]
            if t < 9:
                gmain[t * CH : (t + 1) * CH, :] = val
            else:
                for u in range(4):
                    n = (t - 9) * 4 + u
                    if n < 9:
                        grest[n * CH : (n + 1) * CH, 0:REST] = val[:, u * REST : (u + 1) * REST]

    pack(meta, 1, gproj, gmain, grest, stage, theirs_o)


def pack(meta, flip, gproj, gmain, grest, stage, out):
    stage[...] = jnp.zeros_like(stage)
    for j in range(PIECES // 2):
        for c in range(2):
            d = 2 * j + c
            for w in range(5):
                stage[c, w * PROJ_ROWS : (w + 1) * PROJ_ROWS, :] = gproj[
                    w * CH + d * PROJ_ROWS : w * CH + (d + 1) * PROJ_ROWS, :
                ]
            stage[c, AT_CONV : AT_CONV + CONV_ROWS, :] = gmain[d * CONV_ROWS : (d + 1) * CONV_ROWS, :]
            stage[c, AT_CONV_REST : AT_CONV_REST + QUARTER, :] = jnp.concatenate(
                [
                    grest[d * CONV_ROWS + g * QUARTER : d * CONV_ROWS + (g + 1) * QUARTER, 0:REST]
                    for g in range(4)
                ],
                axis=1,
            )
        out[j] = jnp.where(meta[4] == flip, stage[0], stage[1]).astype(bf16)


def rest_kernel(bucket, sizes, ctx, hid, wo, gproj, gmain, grest, blk_o, mine_o, stage, half):
    meta = place_of(bucket, sizes)
    sy, sx = meta[2], meta[3]
    part = CELLS // 2
    at = pl.multiple_of(sy * part, part)
    half[...] = hid[pl.ds(at, part), :].astype(f32) + dot(ctx[...], wo[...])
    for r in range(TILE_ROWS):
        rows = half[pl.ds(pl.multiple_of(r * COLS + sx * TILE_COLS, 16), TILE_COLS), :]
        cells = sx * TILE_COLS + iota((TILE_COLS, 1), 0)
        keep = (sy * TILE_ROWS + r < meta[0]) & (cells < meta[1])
        blk_o[r * TILE_COLS : (r + 1) * TILE_COLS, :] = jnp.where(keep, rows, 0.0).astype(bf16)
    pack(meta, 0, gproj, gmain, grest, stage, mine_o)


def last_kernel(pieces, conv_o, q_o, k_o, v_o, o_o, total):
    acc = pieces[0].astype(f32)
    for j in range(1, pieces.shape[0]):
        acc = acc + pieces[j].astype(f32)
    total[...] = acc
    conv_o[:MAIN, :] = total[AT_CONV : AT_CONV + CONV_ROWS, :].T
    rest = jnp.concatenate(
        [
            total[AT_CONV_REST : AT_CONV_REST + QUARTER, g * REST : (g + 1) * REST]
            for g in range(4)
        ],
        axis=0,
    )
    conv_o[MAIN:, :] = rest.T
    for w, out in enumerate((q_o, k_o, v_o, o_o)):
        out[:, :MAIN] = total[w * PROJ_ROWS : (w + 1) * PROJ_ROWS, :]
        out[:, MAIN:] = total[AT_PROJ_REST : AT_PROJ_REST + PROJ_ROWS, w * REST : (w + 1) * REST]


VM = pl.BlockSpec(memory_space=pltpu.VMEM)
SM = pl.BlockSpec(memory_space=pltpu.SMEM)
HB = pl.BlockSpec(memory_space=pltpu.HBM)


def shape(dims, dtype):
    return jax.ShapeDtypeStruct(dims, dtype)


def front(sizes, xg, conv_weight, gain):
    flat = (CELLS, CH)
    return pl.pallas_call(
        front_kernel,
        name="front",
        out_shape=[shape(flat, bf16), shape(flat, f32)] + [shape(flat, bf16)] * 2,
        in_specs=[SM, SM] + [VM] * 4 + [HB, VM],
        out_specs=[VM] * 4,
        scratch_shapes=[
            pltpu.VMEM((CELLS + 2 * COLS, 3 * CH), bf16),
            pltpu.VMEM((9 * CH, CH), bf16),
            pltpu.SemaphoreType.DMA((3,)),
        ],
        compiler_params=pltpu.CompilerParams(vmem_limit_bytes=46 * 2**20),
    )(*sizes, *xg, conv_weight, gain)


def back(sizes, og, xin, hid, nrm, pre, gain, wq, wk, wv, wo):
    flat, turned = (CELLS, CH), (CH, CELLS)
    return pl.pallas_call(
        back_kernel,
        name="back",
        out_shape=[
            shape((PIECES // 2, PIECE, 128), bf16),
            shape((CELLS // 2, CH), bf16),
            shape((5 * CH, 128), f32),
            shape((9 * CH, 128), f32),
            shape((9 * CH, 128), f32),
        ],
        in_specs=[SM, SM] + [VM] * 13,
        out_specs=[VM] * 5,
        scratch_shapes=[
            pltpu.VMEM(flat, bf16),
            pltpu.VMEM(flat, bf16),
            pltpu.VMEM(flat, bf16),
            pltpu.VMEM(flat, bf16),
            pltpu.VMEM(flat, bf16),
            pltpu.VMEM(turned, bf16),
            pltpu.VMEM((HEADS * SLOT, CELLS), bf16),
            pltpu.VMEM(turned, bf16),
            pltpu.VMEM(turned, bf16),
            pltpu.VMEM(turned, bf16),
            pltpu.VMEM(flat, bf16),
            pltpu.VMEM(flat, bf16),
            pltpu.VMEM((2, CELLS, 128), bf16),
            pltpu.VMEM(flat, f32),
            pltpu.VMEM(flat, bf16),
            pltpu.VMEM((CELLS, 12 * 128), bf16),
            pltpu.VMEM((3, CELLS + 2 * COLS, 128), bf16),
            pltpu.VMEM((CELLS + 2 * COLS, 3 * 128), f32),
            pltpu.VMEM((2, PIECE, 128), f32),
        ],
        compiler_params=pltpu.CompilerParams(vmem_limit_bytes=32 * 2**20),
    )(*sizes, *og, xin, hid, nrm, pre, gain, wq, wk, wv, wo)


def rest(sizes, ctx, hid, wo, gproj, gmain, grest):
    return pl.pallas_call(
        rest_kernel,
        name="rest",
        out_shape=[
            shape((TILE_ROWS * TILE_COLS, CH), bf16),
            shape((PIECES // 2, PIECE, 128), bf16),
        ],
        in_specs=[SM, SM] + [VM] * 6,
        out_specs=[VM] * 2,
        scratch_shapes=[
            pltpu.VMEM((2, PIECE, 128), f32),
            pltpu.VMEM((CELLS // 2, CH), f32),
        ],
        compiler_params=pltpu.CompilerParams(vmem_limit_bytes=20 * 2**20),
    )(*sizes, ctx, hid, wo, gproj, gmain, grest)


def last(pieces):
    small = shape((PROJ_ROWS, PART), f32)
    return pl.pallas_call(
        last_kernel,
        name="last",
        out_shape=[shape((PART, CONV_ROWS), f32), small, small, small, small],
        in_specs=[VM],
        out_specs=[VM] * 5,
        scratch_shapes=[pltpu.VMEM((PIECE, 128), f32)],
    )(pieces)


def from_ring(own, turn):
    ring = ("sy", "sx")
    ahead = lax.ppermute(own, ring, [(i, (i + 3) % 4) for i in range(4)])
    if turn:
        across = lax.ppermute(ahead, ring, [(i, (i + 3) % 4) for i in range(4)])
    else:
        across = lax.ppermute(own, ring, [(i, (i + 2) % 4) for i in range(4)])
    behind = lax.ppermute(own, ring, [(i, (i + 1) % 4) for i in range(4)])
    return behind, across, ahead


def body(
    features, bucket_ids, bucket_sizes, conv_weight, norm_gain,
    query_weight, key_weight, value_weight, out_weight, out_grad,
):
    sizes = (bucket_ids, bucket_sizes)
    gain = norm_gain.reshape(1, CH)
    x, g = features.reshape(-1, CH), out_grad.reshape(-1, CH)
    xg = (x, *from_ring(x, False))
    og = (g, *from_ring(g, True))
    xin, pre, hid, nrm = front(sizes, xg, conv_weight, gain)
    theirs, ctx, *grads = back(
        sizes, og, xin, hid, nrm, pre, gain, query_weight, key_weight, value_weight, out_weight
    )
    count = lax.axis_size("dp")
    other = lax.ppermute(theirs, "dp", [(i, i ^ 1) for i in range(count)])
    block, mine = rest(sizes, ctx, hid, out_weight, *grads)
    both = (mine.astype(f32) + other.astype(f32)).astype(bf16)
    groups = [[c + 2 * i for i in range(count // 2)] for c in range(2)]
    pieces = lax.all_to_all(both, "dp", 0, 0, tiled=True, axis_index_groups=groups)
    conv_t, *grads = last(pieces)
    return (block.reshape(features.shape), conv_t.T, *grads)


def solution(mesh):
    tiles = P("dp", "sy", "sx", None)
    grad = P("dp", ("sy", "sx"))
    return jax.shard_map(
        body,
        mesh=mesh,
        in_specs=(tiles, P("dp"), P(), P(), P(), P(), P(), P(), P(), tiles),
        out_specs=(tiles, grad, grad, grad, grad, grad),
        check_vma=False,
    )
```

```python
import jax
import jax.numpy as jnp
from jax import lax
from jax.experimental import pallas as pl
from jax.experimental.pallas import tpu as pltpu
from jax.sharding import PartitionSpec as P

HEADS = 10
EPS = 1e-05
LOG2E = 1.4426950408889634
SLOT = 64 + 16
ROWS, COLS, CH = 16, 32, 640
CELLS = ROWS * COLS
TILE_ROWS, TILE_COLS = 8, 16
WIDTH = CH // HEADS
PART = CH // 4
MAIN, REST = 128, 32
PIECES = 32
CONV_ROWS = 9 * CH // PIECES
QUARTER = CONV_ROWS // 4
PROJ_ROWS = CH // PIECES
AT_PROJ_REST = 4 * PROJ_ROWS
AT_CONV = 100
AT_CONV_REST = 280
PIECE = 336

f32 = jnp.float32
bf16 = jnp.bfloat16


def dot(a, b):
    return jnp.dot(a, b, preferred_element_type=f32)


def dot_t(a, b):
    return lax.dot_general(a, b, (((1,), (1,)), ((), ())), preferred_element_type=f32)


def iota(shape, dim):
    return lax.broadcasted_iota(jnp.int32, shape, dim)


def place_of(bucket, sizes):
    core = lax.axis_index("dp") & 1
    b = bucket[0]
    return sizes[b, 0], sizes[b, 1], lax.axis_index("sy"), lax.axis_index("sx"), core


def valid_rows(meta, start, count):
    cell = start + iota((count, 1), 0)
    return ((cell >> 5) < meta[0]) & ((cell & 31) < meta[1])


def place_tiles(meta, tiles, out):
    edge = iota((TILE_COLS, 1), 0)
    for shift, ref in enumerate(tiles):
        tile = (meta[2] * 2 + meta[3] - shift) & 3
        left = (tile & 1) * TILE_COLS
        for r in range(TILE_ROWS):
            row = (tile >> 1) * TILE_ROWS + r
            x = ref[r * TILE_COLS : (r + 1) * TILE_COLS, :]
            x = jnp.where((row < meta[0]) & (left + edge < meta[1]), x, jnp.zeros_like(x))
            out[pl.ds(pl.multiple_of(row * COLS + left, TILE_COLS), TILE_COLS), :] = x


def front_kernel(
    bucket, sizes, xg0, xg1, xg2, xg3, conv_hbm, gain,
    xin_o, pre_o, hid_o, nrm_o,
    taps, conv, sems,
):
    meta = place_of(bucket, sizes)
    third = 3 * CH
    copies = [
        pltpu.make_async_copy(
            conv_hbm.at[pl.ds(i * third, third)], conv.at[pl.ds(i * third, third)], sems.at[i]
        )
        for i in range(3)
    ]
    for copy in copies:
        copy.start()
    taps[0:COLS, :] = jnp.zeros((COLS, third), bf16)
    taps[CELLS + COLS :, :] = jnp.zeros((COLS, third), bf16)
    col = iota((COLS, 1), 0)

    place_tiles(meta, (xg0, xg1, xg2, xg3), xin_o)
    for r in range(ROWS):
        xb = xin_o[r * COLS : (r + 1) * COLS, :]
        x = xb.astype(f32)
        to = slice((r + 1) * COLS, (r + 2) * COLS)
        taps[to, 0:CH] = jnp.where(col == 0, 0.0, pltpu.roll(x, 1, 0)).astype(bf16)
        taps[to, CH : 2 * CH] = xb
        taps[to, 2 * CH :] = jnp.where(col == COLS - 1, 0.0, pltpu.roll(x, COLS - 1, 0)).astype(bf16)
    for dy in range(3):
        copies[dy].wait()
        part = dot(taps[dy * COLS : dy * COLS + CELLS, :], conv[dy * third : (dy + 1) * third, :])
        if dy == 0:
            pre_o[...] = part
        else:
            pre_o[...] += part

    step = 64

    def norm(i, carry):
        at = pl.multiple_of(i * step, step)
        rows = pl.ds(at, step)
        pre = pre_o[rows, :]
        act = pre / (1.0 + jnp.exp(-pre))
        hid = jnp.where(valid_rows(meta, at, step), xin_o[rows, :].astype(f32) + act, 0.0)
        hid = hid.astype(bf16)
        hid_o[rows, :] = hid
        hid = hid.astype(f32)
        centred = hid - jnp.mean(hid, axis=1, keepdims=True)
        spread = jnp.mean(centred * centred, axis=1, keepdims=True)
        nrm_o[rows, :] = (centred * lax.rsqrt(spread + EPS) * gain[...]).astype(bf16)
        return carry

    lax.fori_loop(0, CELLS // step, norm, 0, unroll=True)


def back_kernel(
    bucket, sizes, og0, og1, og2, og3, xin, hid, nrm, pre, gain, wq, wk, wv, wo,
    theirs_o, ctx_o, gproj, gmain, grest,
    q, k, v, gb, gc, kt, vt, gt, ctxt, dqt, dk, dv, bias, dn, dpre, wide, padm, padr, stage,
):
    meta = place_of(bucket, sizes)
    sy, sx = meta[2], meta[3]
    col = iota((COLS, 1), 0)

    place_tiles(meta, (og0, og1, og2, og3), gb)
    normed = nrm[...]
    q[...] = (dot(normed, wq[...]) * (WIDTH**-0.5 * LOG2E)).astype(bf16)
    k[...] = dot(normed, wk[...]).astype(bf16)
    v[...] = dot(normed, wv[...]).astype(bf16)
    gc[...] = dot_t(gb[...], wo[...]).astype(bf16)
    kt[...] = k[...].T
    gt[...] = gc[...].T
    for h in range(HEADS):
        vt[h * SLOT : h * SLOT + WIDTH, :] = v[:, h * WIDTH : (h + 1) * WIDTH].T
        vt[h * SLOT + WIDTH : (h + 1) * SLOT, :] = jnp.ones((SLOT - WIDTH, CELLS), bf16)
    lane = iota((1, 2 * WIDTH), 1)
    ok = valid_rows(meta, 0, CELLS)
    for e in range(2):
        bias[e] = jnp.where((lane == WIDTH * (1 - e)) & ~ok, -1e30, 0.0).astype(bf16)

    def stage_a(h):
        lanes = slice(h // 2 * 2 * WIDTH, (h // 2 + 1) * 2 * WIDTH)
        e = h % 2
        own = (lane >= WIDTH * e) & (lane < WIDTH * (e + 1))
        one = jnp.where(lane == WIDTH * (1 - e), 1.0, 0.0).astype(bf16)
        zero = jnp.zeros((), bf16)
        q2, g2 = q[:, lanes], gc[:, lanes]
        s = dot_t(jnp.where(own, k[:, lanes], bias[e]), jnp.where(own, q2, one))
        return dict(h=h, s=s, qm=jnp.where(own, q2, zero), gm=jnp.where(own, g2, zero))

    def stage_b(t):
        s = t.pop("s")
        t["ex"] = jnp.exp2(s - jnp.max(s, axis=0, keepdims=True))
        t["eb"] = t["ex"].astype(bf16)

    def stage_c(t):
        h = t["h"]
        rows = slice(h * WIDTH, (h + 1) * WIDTH)
        ctx = dot(vt[h * SLOT : (h + 1) * SLOT, :], t["eb"])
        inv = 1.0 / ctx[WIDTH : WIDTH + 1, :]
        ctx = ctx[:WIDTH, :] * inv
        ctxt[rows, :] = ctx.astype(bf16)
        t["delta"] = jnp.sum(gt[rows, :].astype(f32) * ctx, axis=0, keepdims=True)
        t["inv"] = inv

    def stage_d(t):
        h = t["h"]
        lanes = slice(h // 2 * 2 * WIDTH, (h // 2 + 1) * 2 * WIDTH)
        t["dp"] = dot_t(v[:, lanes], t["gm"])
        t["ds"] = (t.pop("ex") * (t.pop("dp") - t.pop("delta"))).astype(bf16)

    def stage_e(t):
        h, ds, inv = t["h"], t.pop("ds"), t.pop("inv")
        rows = slice(h * WIDTH, (h + 1) * WIDTH)
        dqt[rows, :] = (dot(kt[rows, :], ds) * (inv * WIDTH**-0.5)).astype(bf16)
        col = jnp.broadcast_to(inv, (8, CELLS)).T[:, 0:1]
        t["dk"] = dot(ds, (t.pop("qm").astype(f32) * col).astype(bf16))
        t["dv"] = dot(t.pop("eb"), (t.pop("gm").astype(f32) * col).astype(bf16))

    def stage_f(t, u):
        lanes = slice(t["h"] * WIDTH, (t["h"] + 2) * WIDTH)
        dk[:, lanes] = ((t["dk"] + u["dk"]) * (1.0 / LOG2E)).astype(bf16)
        dv[:, lanes] = (t["dv"] + u["dv"]).astype(bf16)


    heads = [stage_a(0)]
    for h in range(HEADS + 1):
        if h + 1 < HEADS:
            heads.append(stage_a(h + 1))
        if h < HEADS:
            stage_b(heads[h])
        if h > 0:
            stage_e(heads[h - 1])
        if h < HEADS:
            stage_c(heads[h])
            stage_d(heads[h])
        if h > 0 and h % 2 == 0:
            stage_f(heads[h - 2], heads[h - 1])
    ctx_o[...] = ctxt[:, pl.ds(pl.multiple_of(sy * (CELLS // 2), CELLS // 2), CELLS // 2)].T
    dq = dqt[...].T
    dn[...] = dot_t(dq, wq[...]) + dot_t(dk[...], wk[...]) + dot_t(dv[...], wv[...])
    step = 64

    def norm_back(i, carry):
        at = pl.multiple_of(i * step, step)
        rows = pl.ds(at, step)
        h = hid[rows, :].astype(f32)
        centred = h - jnp.mean(h, axis=1, keepdims=True)
        rstd = lax.rsqrt(jnp.mean(centred * centred, axis=1, keepdims=True) + EPS)
        xhat = centred * rstd
        dx = dn[rows, :] * gain[...]
        m1 = jnp.mean(dx, axis=1, keepdims=True)
        m2 = jnp.mean(dx * xhat, axis=1, keepdims=True)
        dh = gb[rows, :].astype(f32) + rstd * (dx - m1 - xhat * m2)
        a = pre[rows, :]
        sig = 1.0 / (1.0 + jnp.exp(-a))
        out = dh * sig * (1.0 + a * (1.0 - sig))
        dpre[rows, :] = jnp.where(valid_rows(meta, at, step), out, 0.0).astype(bf16)
        return carry

    lax.fori_loop(0, CELLS // step, norm_back, 0, unroll=True)

    first = (sy * 2 + sx) * PART
    row = iota((CH, 1), 0) - first

    def pick(lo, lanes, group=None):
        n = iota((1, lanes), 1)
        want = n + lo if group is None else (n & (REST - 1)) + lo
        hit = row == want
        if group is not None and group >= 0:
            hit = hit & ((n >> 5) == group)
        return jnp.where(hit, 1.0, 0.0).astype(bf16)

    nt = nrm[...].T
    main = pick(0, MAIN)
    grads = (dq, dk[...], dv[...], gb[...])
    mains, rests = [], []
    for w, g in enumerate(grads):
        both = dot(g, jnp.concatenate([main, pick(MAIN, 4 * REST, w)], axis=1))
        mains.append(both[:, :MAIN].astype(bf16))
        rests.append(both[:, MAIN:])
    qkv = dot(nt, jnp.concatenate(mains[:3] + [(rests[0] + rests[1] + rests[2]).astype(bf16)], axis=1))
    out = dot(ctxt[...], jnp.concatenate([mains[3], rests[3].astype(bf16)], axis=1))
    for w in range(3):
        gproj[w * CH : (w + 1) * CH, :] = qkv[:, w * MAIN : (w + 1) * MAIN]
    gproj[3 * CH : 4 * CH, :] = out[:, :MAIN]
    gproj[4 * CH :, :] = qkv[:, 3 * MAIN :] + out[:, MAIN:]

    ccol = iota((CELLS, 1), 0) & (COLS - 1)
    dmain = dot(dpre[...], main)
    drest = dot(dpre[...], pick(MAIN, 3 * MAIN, -1))
    up = lambda x: jnp.where(ccol == COLS - 1, 0.0, pltpu.roll(x, CELLS - 1, 0))
    down = lambda x: jnp.where(ccol == 0, 0.0, pltpu.roll(x, 1, 0))
    padm[...] = jnp.zeros_like(padm)
    padr[...] = jnp.zeros_like(padr)
    inner = slice(COLS, COLS + CELLS)
    padm[0, inner, :] = up(dmain).astype(bf16)
    padm[1, inner, :] = dmain.astype(bf16)
    padm[2, inner, :] = down(dmain).astype(bf16)
    tap = iota((1, 3 * MAIN), 1) >> 5
    tap_dx = tap % 3
    tap_dy = tap // 3
    padr[inner, :] = jnp.where(tap_dx == 0, up(drest), jnp.where(tap_dx == 1, drest, down(drest)))
    for t in range(9):
        lo = (2 - t // 3) * COLS
        wide[:, t * MAIN : (t + 1) * MAIN] = padm[t % 3, lo : lo + CELLS, :]
    wide[:, 9 * MAIN :] = jnp.where(
        tap_dy == 0,
        padr[2 * COLS :, :],
        jnp.where(tap_dy == 1, padr[inner, :], padr[0:CELLS, :]),
    ).astype(bf16)
    xt = xin[...].T
    for j in range(6):
        g = dot(xt, wide[:, j * 256 : (j + 1) * 256])
        for i in range(2):
            t = 2 * j + i
            val = g[:, i * MAIN : (i + 1) * MAIN]
            if t < 9:
                gmain[t * CH : (t + 1) * CH, :] = val
            else:
                for u in range(4):
                    n = (t - 9) * 4 + u
                    if n < 9:
                        grest[n * CH : (n + 1) * CH, 0:REST] = val[:, u * REST : (u + 1) * REST]

    pack(meta, 1, gproj, gmain, grest, stage, theirs_o)


def pack(meta, flip, gproj, gmain, grest, stage, out):
    stage[...] = jnp.zeros_like(stage)
    side = meta[4] ^ flip
    for j in range(PIECES // 2):
        d = 2 * j + side
        for w in range(5):
            stage[w * PROJ_ROWS : (w + 1) * PROJ_ROWS, :] = gproj[
                pl.ds(w * CH + d * PROJ_ROWS, PROJ_ROWS), :
            ]
        first = d * CONV_ROWS
        stage[AT_CONV : AT_CONV + CONV_ROWS, :] = gmain[pl.ds(first, CONV_ROWS), :]
        stage[AT_CONV_REST : AT_CONV_REST + QUARTER, :] = jnp.concatenate(
            [grest[pl.ds(first + g * QUARTER, QUARTER), 0:REST] for g in range(4)], axis=1
        )
        out[j] = stage[...].astype(bf16)


def rest_kernel(bucket, sizes, ctx, hid, wo, gproj, gmain, grest, blk_o, mine_o, stage, half):
    meta = place_of(bucket, sizes)
    sy, sx = meta[2], meta[3]
    part = CELLS // 2
    at = pl.multiple_of(sy * part, part)
    half[...] = hid[pl.ds(at, part), :].astype(f32) + dot(ctx[...], wo[...])
    for r in range(TILE_ROWS):
        rows = half[pl.ds(pl.multiple_of(r * COLS + sx * TILE_COLS, 16), TILE_COLS), :]
        cells = sx * TILE_COLS + iota((TILE_COLS, 1), 0)
        keep = (sy * TILE_ROWS + r < meta[0]) & (cells < meta[1])
        blk_o[r * TILE_COLS : (r + 1) * TILE_COLS, :] = jnp.where(keep, rows, 0.0).astype(bf16)
    pack(meta, 0, gproj, gmain, grest, stage, mine_o)


def last_kernel(pieces, conv_o, q_o, k_o, v_o, o_o, total):
    acc = pieces[0].astype(f32)
    for j in range(1, pieces.shape[0]):
        acc = acc + pieces[j].astype(f32)
    total[...] = acc
    conv_o[:MAIN, :] = total[AT_CONV : AT_CONV + CONV_ROWS, :].T
    rest = jnp.concatenate(
        [
            total[AT_CONV_REST : AT_CONV_REST + QUARTER, g * REST : (g + 1) * REST]
            for g in range(4)
        ],
        axis=0,
    )
    conv_o[MAIN:, :] = rest.T
    for w, out in enumerate((q_o, k_o, v_o, o_o)):
        out[:, :MAIN] = total[w * PROJ_ROWS : (w + 1) * PROJ_ROWS, :]
        out[:, MAIN:] = total[AT_PROJ_REST : AT_PROJ_REST + PROJ_ROWS, w * REST : (w + 1) * REST]


VM = pl.BlockSpec(memory_space=pltpu.VMEM)
SM = pl.BlockSpec(memory_space=pltpu.SMEM)
HB = pl.BlockSpec(memory_space=pltpu.HBM)


def shape(dims, dtype):
    return jax.ShapeDtypeStruct(dims, dtype)


def front(sizes, xg, conv_weight, gain):
    flat = (CELLS, CH)
    return pl.pallas_call(
        front_kernel,
        name="front",
        out_shape=[shape(flat, bf16), shape(flat, f32)] + [shape(flat, bf16)] * 2,
        in_specs=[SM, SM] + [VM] * 4 + [HB, VM],
        out_specs=[VM] * 4,
        scratch_shapes=[
            pltpu.VMEM((CELLS + 2 * COLS, 3 * CH), bf16),
            pltpu.VMEM((9 * CH, CH), bf16),
            pltpu.SemaphoreType.DMA((3,)),
        ],
        compiler_params=pltpu.CompilerParams(vmem_limit_bytes=46 * 2**20),
    )(*sizes, *xg, conv_weight, gain)


def back(sizes, og, xin, hid, nrm, pre, gain, wq, wk, wv, wo):
    flat, turned = (CELLS, CH), (CH, CELLS)
    return pl.pallas_call(
        back_kernel,
        name="back",
        out_shape=[
            shape((PIECES // 2, PIECE, 128), bf16),
            shape((CELLS // 2, CH), bf16),
            shape((5 * CH, 128), f32),
            shape((9 * CH, 128), f32),
            shape((9 * CH, 128), f32),
        ],
        in_specs=[SM, SM] + [VM] * 13,
        out_specs=[VM] * 5,
        scratch_shapes=[
            pltpu.VMEM(flat, bf16),
            pltpu.VMEM(flat, bf16),
            pltpu.VMEM(flat, bf16),
            pltpu.VMEM(flat, bf16),
            pltpu.VMEM(flat, bf16),
            pltpu.VMEM(turned, bf16),
            pltpu.VMEM((HEADS * SLOT, CELLS), bf16),
            pltpu.VMEM(turned, bf16),
            pltpu.VMEM(turned, bf16),
            pltpu.VMEM(turned, bf16),
            pltpu.VMEM(flat, bf16),
            pltpu.VMEM(flat, bf16),
            pltpu.VMEM((2, CELLS, 128), bf16),
            pltpu.VMEM(flat, f32),
            pltpu.VMEM(flat, bf16),
            pltpu.VMEM((CELLS, 12 * 128), bf16),
            pltpu.VMEM((3, CELLS + 2 * COLS, 128), bf16),
            pltpu.VMEM((CELLS + 2 * COLS, 3 * 128), f32),
            pltpu.VMEM((PIECE, 128), f32),
        ],
        compiler_params=pltpu.CompilerParams(vmem_limit_bytes=32 * 2**20),
    )(*sizes, *og, xin, hid, nrm, pre, gain, wq, wk, wv, wo)


def rest(sizes, ctx, hid, wo, gproj, gmain, grest):
    return pl.pallas_call(
        rest_kernel,
        name="rest",
        out_shape=[
            shape((TILE_ROWS * TILE_COLS, CH), bf16),
            shape((PIECES // 2, PIECE, 128), bf16),
        ],
        in_specs=[SM, SM] + [VM] * 6,
        out_specs=[VM] * 2,
        scratch_shapes=[
            pltpu.VMEM((PIECE, 128), f32),
            pltpu.VMEM((CELLS // 2, CH), f32),
        ],
        compiler_params=pltpu.CompilerParams(vmem_limit_bytes=20 * 2**20),
    )(*sizes, ctx, hid, wo, gproj, gmain, grest)


def last(pieces):
    small = shape((PROJ_ROWS, PART), f32)
    return pl.pallas_call(
        last_kernel,
        name="last",
        out_shape=[shape((PART, CONV_ROWS), f32), small, small, small, small],
        in_specs=[VM],
        out_specs=[VM] * 5,
        scratch_shapes=[pltpu.VMEM((PIECE, 128), f32)],
    )(pieces)


def from_ring(own, turn):
    ring = ("sy", "sx")
    ahead = lax.ppermute(own, ring, [(i, (i + 3) % 4) for i in range(4)])
    if turn:
        across = lax.ppermute(ahead, ring, [(i, (i + 3) % 4) for i in range(4)])
    else:
        across = lax.ppermute(own, ring, [(i, (i + 2) % 4) for i in range(4)])
    behind = lax.ppermute(own, ring, [(i, (i + 1) % 4) for i in range(4)])
    return behind, across, ahead


def body(
    features, bucket_ids, bucket_sizes, conv_weight, norm_gain,
    query_weight, key_weight, value_weight, out_weight, out_grad,
):
    sizes = (bucket_ids, bucket_sizes)
    gain = norm_gain.reshape(1, CH)
    x, g = features.reshape(-1, CH), out_grad.reshape(-1, CH)
    xg = (x, *from_ring(x, False))
    og = (g, *from_ring(g, True))
    xin, pre, hid, nrm = front(sizes, xg, conv_weight, gain)
    theirs, ctx, *grads = back(
        sizes, og, xin, hid, nrm, pre, gain, query_weight, key_weight, value_weight, out_weight
    )
    count = lax.axis_size("dp")
    other = lax.ppermute(theirs, "dp", [(i, i ^ 1) for i in range(count)])
    block, mine = rest(sizes, ctx, hid, out_weight, *grads)
    both = (mine.astype(f32) + other.astype(f32)).astype(bf16)
    groups = [[c + 2 * i for i in range(count // 2)] for c in range(2)]
    pieces = lax.all_to_all(both, "dp", 0, 0, tiled=True, axis_index_groups=groups)
    conv_t, *grads = last(pieces)
    return (block.reshape(features.shape), conv_t.T, *grads)


def solution(mesh):
    tiles = P("dp", "sy", "sx", None)
    grad = P("dp", ("sy", "sx"))
    return jax.shard_map(
        body,
        mesh=mesh,
        in_specs=(tiles, P("dp"), P(), P(), P(), P(), P(), P(), P(), tiles),
        out_specs=(tiles, grad, grad, grad, grad, grad),
        check_vma=False,
    )
```

```python
import jax
import jax.numpy as jnp
from jax import lax
from jax.experimental import pallas as pl
from jax.experimental.pallas import tpu as pltpu
from jax.sharding import PartitionSpec as P

HEADS = 10
EPS = 1e-05
LOG2E = 1.4426950408889634
SLOT = 64 + 16
ROWS, COLS, CH = 16, 32, 640
CELLS = ROWS * COLS
TILE_ROWS, TILE_COLS = 8, 16
WIDTH = CH // HEADS
PART = CH // 4
MAIN, REST = 128, 32
PIECES = 32
CONV_ROWS = 9 * CH // PIECES
QUARTER = CONV_ROWS // 4
PROJ_ROWS = CH // PIECES
AT_PROJ_REST = 4 * PROJ_ROWS
AT_CONV = 100
AT_CONV_REST = 280
PIECE = 336

f32 = jnp.float32
bf16 = jnp.bfloat16


def dot(a, b):
    return jnp.dot(a, b, preferred_element_type=f32)


def dot_t(a, b):
    return lax.dot_general(a, b, (((1,), (1,)), ((), ())), preferred_element_type=f32)


def iota(shape, dim):
    return lax.broadcasted_iota(jnp.int32, shape, dim)


def place_of(bucket, sizes):
    core = lax.axis_index("dp") & 1
    b = bucket[0]
    return sizes[b, 0], sizes[b, 1], lax.axis_index("sy"), lax.axis_index("sx"), core


def valid_rows(meta, start, count):
    cell = start + iota((count, 1), 0)
    return ((cell >> 5) < meta[0]) & ((cell & 31) < meta[1])


def place_tiles(meta, tiles, out):
    edge = iota((TILE_COLS, 1), 0)
    for shift, ref in enumerate(tiles):
        tile = (meta[2] * 2 + meta[3] - shift) & 3
        left = (tile & 1) * TILE_COLS
        for r in range(TILE_ROWS):
            row = (tile >> 1) * TILE_ROWS + r
            x = ref[r * TILE_COLS : (r + 1) * TILE_COLS, :]
            x = jnp.where((row < meta[0]) & (left + edge < meta[1]), x, jnp.zeros_like(x))
            out[pl.ds(pl.multiple_of(row * COLS + left, TILE_COLS), TILE_COLS), :] = x


def front_kernel(
    bucket, sizes, xg0, xg1, xg2, xg3, conv_hbm, gain,
    xin_o, pre_o, hid_o, nrm_o,
    taps, conv, sems,
):
    meta = place_of(bucket, sizes)
    third = 3 * CH
    copies = [
        pltpu.make_async_copy(
            conv_hbm.at[pl.ds(i * third, third)], conv.at[pl.ds(i * third, third)], sems.at[i]
        )
        for i in range(3)
    ]
    for copy in copies:
        copy.start()
    taps[0:COLS, :] = jnp.zeros((COLS, third), bf16)
    taps[CELLS + COLS :, :] = jnp.zeros((COLS, third), bf16)
    col = iota((COLS, 1), 0)

    place_tiles(meta, (xg0, xg1, xg2, xg3), xin_o)
    for r in range(ROWS):
        xb = xin_o[r * COLS : (r + 1) * COLS, :]
        x = xb.astype(f32)
        to = slice((r + 1) * COLS, (r + 2) * COLS)
        taps[to, 0:CH] = jnp.where(col == 0, 0.0, pltpu.roll(x, 1, 0)).astype(bf16)
        taps[to, CH : 2 * CH] = xb
        taps[to, 2 * CH :] = jnp.where(col == COLS - 1, 0.0, pltpu.roll(x, COLS - 1, 0)).astype(bf16)
    for dy in range(3):
        copies[dy].wait()
        part = dot(taps[dy * COLS : dy * COLS + CELLS, :], conv[dy * third : (dy + 1) * third, :])
        if dy == 0:
            pre_o[...] = part
        else:
            pre_o[...] += part

    step = 64

    def norm(i, carry):
        at = pl.multiple_of(i * step, step)
        rows = pl.ds(at, step)
        pre = pre_o[rows, :]
        act = pre / (1.0 + jnp.exp(-pre))
        hid = jnp.where(valid_rows(meta, at, step), xin_o[rows, :].astype(f32) + act, 0.0)
        hid = hid.astype(bf16)
        hid_o[rows, :] = hid
        hid = hid.astype(f32)
        centred = hid - jnp.mean(hid, axis=1, keepdims=True)
        spread = jnp.mean(centred * centred, axis=1, keepdims=True)
        nrm_o[rows, :] = (centred * lax.rsqrt(spread + EPS) * gain[...]).astype(bf16)
        return carry

    lax.fori_loop(0, CELLS // step, norm, 0, unroll=True)


def back_kernel(
    bucket, sizes, og0, og1, og2, og3, xin, hid, nrm, pre, gain, wq, wk, wv, wo,
    theirs_o, ctx_o, gproj, gmain, grest,
    q, k, v, gb, gc, kt, vt, gt, ctxt, dqt, dk, dv, bias, dn, dpre, wide, padm, padr, stage,
):
    meta = place_of(bucket, sizes)
    sy, sx = meta[2], meta[3]
    col = iota((COLS, 1), 0)

    place_tiles(meta, (og0, og1, og2, og3), gb)
    normed = nrm[...]
    q[...] = (dot(normed, wq[...]) * (WIDTH**-0.5 * LOG2E)).astype(bf16)
    k[...] = dot(normed, wk[...]).astype(bf16)
    v[...] = dot(normed, wv[...]).astype(bf16)
    gc[...] = dot_t(gb[...], wo[...]).astype(bf16)
    kt[...] = k[...].T
    gt[...] = gc[...].T
    for h in range(HEADS):
        vt[h * SLOT : h * SLOT + WIDTH, :] = v[:, h * WIDTH : (h + 1) * WIDTH].T
        vt[h * SLOT + WIDTH : (h + 1) * SLOT, :] = jnp.ones((SLOT - WIDTH, CELLS), bf16)
    lane = iota((1, 2 * WIDTH), 1)
    ok = valid_rows(meta, 0, CELLS)
    for e in range(2):
        bias[e] = jnp.where((lane == WIDTH * (1 - e)) & ~ok, -1e30, 0.0).astype(bf16)

    def stage_a(h):
        lanes = slice(h // 2 * 2 * WIDTH, (h // 2 + 1) * 2 * WIDTH)
        e = h % 2
        own = (lane >= WIDTH * e) & (lane < WIDTH * (e + 1))
        one = jnp.where(lane == WIDTH * (1 - e), 1.0, 0.0).astype(bf16)
        zero = jnp.zeros((), bf16)
        q2, g2 = q[:, lanes], gc[:, lanes]
        s = dot_t(jnp.where(own, k[:, lanes], bias[e]), jnp.where(own, q2, one))
        return dict(h=h, s=s, qm=jnp.where(own, q2, zero), gm=jnp.where(own, g2, zero))

    def stage_b(t):
        s = t.pop("s")
        t["ex"] = jnp.exp2(s - jnp.max(s, axis=0, keepdims=True))
        t["eb"] = t["ex"].astype(bf16)

    def stage_c(t):
        h = t["h"]
        rows = slice(h * WIDTH, (h + 1) * WIDTH)
        ctx = dot(vt[h * SLOT : (h + 1) * SLOT, :], t["eb"])
        inv = 1.0 / ctx[WIDTH : WIDTH + 1, :]
        ctx = ctx[:WIDTH, :] * inv
        ctxt[rows, :] = ctx.astype(bf16)
        t["delta"] = jnp.sum(gt[rows, :].astype(f32) * ctx, axis=0, keepdims=True)
        t["inv"] = inv

    def stage_p(t):
        h = t["h"]
        lanes = slice(h // 2 * 2 * WIDTH, (h // 2 + 1) * 2 * WIDTH)
        t["dp"] = dot_t(v[:, lanes], t["gm"])

    def stage_d(t):
        t["ds"] = (t.pop("ex") * (t.pop("dp") - t.pop("delta"))).astype(bf16)

    def stage_e(t):
        h, ds, inv = t["h"], t.pop("ds"), t.pop("inv")
        rows = slice(h * WIDTH, (h + 1) * WIDTH)
        dqt[rows, :] = (dot(kt[rows, :], ds) * (inv * WIDTH**-0.5)).astype(bf16)
        col = jnp.broadcast_to(inv, (8, CELLS)).T[:, 0:1]
        t["dk"] = dot(ds, (t.pop("qm").astype(f32) * col).astype(bf16))
        t["dv"] = dot(t.pop("eb"), (t.pop("gm").astype(f32) * col).astype(bf16))

    def stage_f(t, u):
        lanes = slice(t["h"] * WIDTH, (t["h"] + 2) * WIDTH)
        dk[:, lanes] = ((t["dk"] + u["dk"]) * (1.0 / LOG2E)).astype(bf16)
        dv[:, lanes] = (t["dv"] + u["dv"]).astype(bf16)


    heads = [stage_a(0)]
    for h in range(HEADS + 1):
        if h < HEADS:
            stage_b(heads[h])
        if h > 0:
            stage_e(heads[h - 1])
        if h < HEADS:
            stage_c(heads[h])
            stage_p(heads[h])
        if h + 1 < HEADS:
            heads.append(stage_a(h + 1))
        if h < HEADS:
            stage_d(heads[h])
        if h > 0 and h % 2 == 0:
            stage_f(heads[h - 2], heads[h - 1])
    ctx_o[...] = ctxt[:, pl.ds(pl.multiple_of(sy * (CELLS // 2), CELLS // 2), CELLS // 2)].T
    dq = dqt[...].T
    dn[...] = dot_t(dq, wq[...]) + dot_t(dk[...], wk[...]) + dot_t(dv[...], wv[...])
    step = 64

    def norm_back(i, carry):
        at = pl.multiple_of(i * step, step)
        rows = pl.ds(at, step)
        h = hid[rows, :].astype(f32)
        centred = h - jnp.mean(h, axis=1, keepdims=True)
        rstd = lax.rsqrt(jnp.mean(centred * centred, axis=1, keepdims=True) + EPS)
        xhat = centred * rstd
        dx = dn[rows, :] * gain[...]
        m1 = jnp.mean(dx, axis=1, keepdims=True)
        m2 = jnp.mean(dx * xhat, axis=1, keepdims=True)
        dh = gb[rows, :].astype(f32) + rstd * (dx - m1 - xhat * m2)
        a = pre[rows, :]
        sig = 1.0 / (1.0 + jnp.exp(-a))
        out = dh * sig * (1.0 + a * (1.0 - sig))
        dpre[rows, :] = jnp.where(valid_rows(meta, at, step), out, 0.0).astype(bf16)
        return carry

    lax.fori_loop(0, CELLS // step, norm_back, 0, unroll=True)

    first = (sy * 2 + sx) * PART
    row = iota((CH, 1), 0) - first

    def pick(lo, lanes, group=None):
        n = iota((1, lanes), 1)
        want = n + lo if group is None else (n & (REST - 1)) + lo
        hit = row == want
        if group is not None and group >= 0:
            hit = hit & ((n >> 5) == group)
        return jnp.where(hit, 1.0, 0.0).astype(bf16)

    nt = nrm[...].T
    main = pick(0, MAIN)
    grads = (dq, dk[...], dv[...], gb[...])
    mains, rests = [], []
    for w, g in enumerate(grads):
        both = dot(g, jnp.concatenate([main, pick(MAIN, 4 * REST, w)], axis=1))
        mains.append(both[:, :MAIN].astype(bf16))
        rests.append(both[:, MAIN:])
    qkv = dot(nt, jnp.concatenate(mains[:3] + [(rests[0] + rests[1] + rests[2]).astype(bf16)], axis=1))
    out = dot(ctxt[...], jnp.concatenate([mains[3], rests[3].astype(bf16)], axis=1))
    for w in range(3):
        gproj[w * CH : (w + 1) * CH, :] = qkv[:, w * MAIN : (w + 1) * MAIN]
    gproj[3 * CH : 4 * CH, :] = out[:, :MAIN]
    gproj[4 * CH :, :] = qkv[:, 3 * MAIN :] + out[:, MAIN:]

    ccol = iota((CELLS, 1), 0) & (COLS - 1)
    dmain = dot(dpre[...], main)
    drest = dot(dpre[...], pick(MAIN, 3 * MAIN, -1))
    up = lambda x: jnp.where(ccol == COLS - 1, 0.0, pltpu.roll(x, CELLS - 1, 0))
    down = lambda x: jnp.where(ccol == 0, 0.0, pltpu.roll(x, 1, 0))
    padm[...] = jnp.zeros_like(padm)
    padr[...] = jnp.zeros_like(padr)
    inner = slice(COLS, COLS + CELLS)
    padm[0, inner, :] = up(dmain).astype(bf16)
    padm[1, inner, :] = dmain.astype(bf16)
    padm[2, inner, :] = down(dmain).astype(bf16)
    tap = iota((1, 3 * MAIN), 1) >> 5
    tap_dx = tap % 3
    tap_dy = tap // 3
    padr[inner, :] = jnp.where(tap_dx == 0, up(drest), jnp.where(tap_dx == 1, drest, down(drest)))
    for t in range(9):
        lo = (2 - t // 3) * COLS
        wide[:, t * MAIN : (t + 1) * MAIN] = padm[t % 3, lo : lo + CELLS, :]
    wide[:, 9 * MAIN :] = jnp.where(
        tap_dy == 0,
        padr[2 * COLS :, :],
        jnp.where(tap_dy == 1, padr[inner, :], padr[0:CELLS, :]),
    ).astype(bf16)
    xt = xin[...].T
    for j in range(6):
        g = dot(xt, wide[:, j * 256 : (j + 1) * 256])
        for i in range(2):
            t = 2 * j + i
            val = g[:, i * MAIN : (i + 1) * MAIN]
            if t < 9:
                gmain[t * CH : (t + 1) * CH, :] = val
            else:
                for u in range(4):
                    n = (t - 9) * 4 + u
                    if n < 9:
                        grest[n * CH : (n + 1) * CH, 0:REST] = val[:, u * REST : (u + 1) * REST]

    pack(meta, 1, gproj, gmain, grest, stage, theirs_o)


def pack(meta, flip, gproj, gmain, grest, stage, out):
    stage[...] = jnp.zeros_like(stage)
    side = meta[4] ^ flip
    for j in range(PIECES // 2):
        d = 2 * j + side
        for w in range(5):
            stage[w * PROJ_ROWS : (w + 1) * PROJ_ROWS, :] = gproj[
                pl.ds(w * CH + d * PROJ_ROWS, PROJ_ROWS), :
            ]
        first = d * CONV_ROWS
        stage[AT_CONV : AT_CONV + CONV_ROWS, :] = gmain[pl.ds(first, CONV_ROWS), :]
        stage[AT_CONV_REST : AT_CONV_REST + QUARTER, :] = jnp.concatenate(
            [grest[pl.ds(first + g * QUARTER, QUARTER), 0:REST] for g in range(4)], axis=1
        )
        out[j] = stage[...].astype(bf16)


def rest_kernel(bucket, sizes, ctx, hid, wo, gproj, gmain, grest, blk_o, mine_o, stage, half):
    meta = place_of(bucket, sizes)
    sy, sx = meta[2], meta[3]
    part = CELLS // 2
    at = pl.multiple_of(sy * part, part)
    half[...] = hid[pl.ds(at, part), :].astype(f32) + dot(ctx[...], wo[...])
    for r in range(TILE_ROWS):
        rows = half[pl.ds(pl.multiple_of(r * COLS + sx * TILE_COLS, 16), TILE_COLS), :]
        cells = sx * TILE_COLS + iota((TILE_COLS, 1), 0)
        keep = (sy * TILE_ROWS + r < meta[0]) & (cells < meta[1])
        blk_o[r * TILE_COLS : (r + 1) * TILE_COLS, :] = jnp.where(keep, rows, 0.0).astype(bf16)
    pack(meta, 0, gproj, gmain, grest, stage, mine_o)


def last_kernel(pieces, conv_o, q_o, k_o, v_o, o_o, total):
    acc = pieces[0].astype(f32)
    for j in range(1, pieces.shape[0]):
        acc = acc + pieces[j].astype(f32)
    total[...] = acc
    conv_o[:MAIN, :] = total[AT_CONV : AT_CONV + CONV_ROWS, :].T
    rest = jnp.concatenate(
        [
            total[AT_CONV_REST : AT_CONV_REST + QUARTER, g * REST : (g + 1) * REST]
            for g in range(4)
        ],
        axis=0,
    )
    conv_o[MAIN:, :] = rest.T
    for w, out in enumerate((q_o, k_o, v_o, o_o)):
        out[:, :MAIN] = total[w * PROJ_ROWS : (w + 1) * PROJ_ROWS, :]
        out[:, MAIN:] = total[AT_PROJ_REST : AT_PROJ_REST + PROJ_ROWS, w * REST : (w + 1) * REST]


VM = pl.BlockSpec(memory_space=pltpu.VMEM)
SM = pl.BlockSpec(memory_space=pltpu.SMEM)
HB = pl.BlockSpec(memory_space=pltpu.HBM)


def shape(dims, dtype):
    return jax.ShapeDtypeStruct(dims, dtype)


def front(sizes, xg, conv_weight, gain):
    flat = (CELLS, CH)
    return pl.pallas_call(
        front_kernel,
        name="front",
        out_shape=[shape(flat, bf16), shape(flat, f32)] + [shape(flat, bf16)] * 2,
        in_specs=[SM, SM] + [VM] * 4 + [HB, VM],
        out_specs=[VM] * 4,
        scratch_shapes=[
            pltpu.VMEM((CELLS + 2 * COLS, 3 * CH), bf16),
            pltpu.VMEM((9 * CH, CH), bf16),
            pltpu.SemaphoreType.DMA((3,)),
        ],
        compiler_params=pltpu.CompilerParams(vmem_limit_bytes=46 * 2**20),
    )(*sizes, *xg, conv_weight, gain)


def back(sizes, og, xin, hid, nrm, pre, gain, wq, wk, wv, wo):
    flat, turned = (CELLS, CH), (CH, CELLS)
    return pl.pallas_call(
        back_kernel,
        name="back",
        out_shape=[
            shape((PIECES // 2, PIECE, 128), bf16),
            shape((CELLS // 2, CH), bf16),
            shape((5 * CH, 128), f32),
            shape((9 * CH, 128), f32),
            shape((9 * CH, 128), f32),
        ],
        in_specs=[SM, SM] + [VM] * 13,
        out_specs=[VM] * 5,
        scratch_shapes=[
            pltpu.VMEM(flat, bf16),
            pltpu.VMEM(flat, bf16),
            pltpu.VMEM(flat, bf16),
            pltpu.VMEM(flat, bf16),
            pltpu.VMEM(flat, bf16),
            pltpu.VMEM(turned, bf16),
            pltpu.VMEM((HEADS * SLOT, CELLS), bf16),
            pltpu.VMEM(turned, bf16),
            pltpu.VMEM(turned, bf16),
            pltpu.VMEM(turned, bf16),
            pltpu.VMEM(flat, bf16),
            pltpu.VMEM(flat, bf16),
            pltpu.VMEM((2, CELLS, 128), bf16),
            pltpu.VMEM(flat, f32),
            pltpu.VMEM(flat, bf16),
            pltpu.VMEM((CELLS, 12 * 128), bf16),
            pltpu.VMEM((3, CELLS + 2 * COLS, 128), bf16),
            pltpu.VMEM((CELLS + 2 * COLS, 3 * 128), f32),
            pltpu.VMEM((PIECE, 128), f32),
        ],
        compiler_params=pltpu.CompilerParams(vmem_limit_bytes=32 * 2**20),
    )(*sizes, *og, xin, hid, nrm, pre, gain, wq, wk, wv, wo)


def rest(sizes, ctx, hid, wo, gproj, gmain, grest):
    return pl.pallas_call(
        rest_kernel,
        name="rest",
        out_shape=[
            shape((TILE_ROWS * TILE_COLS, CH), bf16),
            shape((PIECES // 2, PIECE, 128), bf16),
        ],
        in_specs=[SM, SM] + [VM] * 6,
        out_specs=[VM] * 2,
        scratch_shapes=[
            pltpu.VMEM((PIECE, 128), f32),
            pltpu.VMEM((CELLS // 2, CH), f32),
        ],
        compiler_params=pltpu.CompilerParams(vmem_limit_bytes=20 * 2**20),
    )(*sizes, ctx, hid, wo, gproj, gmain, grest)


def last(pieces):
    small = shape((PROJ_ROWS, PART), f32)
    return pl.pallas_call(
        last_kernel,
        name="last",
        out_shape=[shape((PART, CONV_ROWS), f32), small, small, small, small],
        in_specs=[VM],
        out_specs=[VM] * 5,
        scratch_shapes=[pltpu.VMEM((PIECE, 128), f32)],
    )(pieces)


def from_ring(own, turn):
    ring = ("sy", "sx")
    ahead = lax.ppermute(own, ring, [(i, (i + 3) % 4) for i in range(4)])
    if turn:
        across = lax.ppermute(ahead, ring, [(i, (i + 3) % 4) for i in range(4)])
    else:
        across = lax.ppermute(own, ring, [(i, (i + 2) % 4) for i in range(4)])
    behind = lax.ppermute(own, ring, [(i, (i + 1) % 4) for i in range(4)])
    return behind, across, ahead


def body(
    features, bucket_ids, bucket_sizes, conv_weight, norm_gain,
    query_weight, key_weight, value_weight, out_weight, out_grad,
):
    sizes = (bucket_ids, bucket_sizes)
    gain = norm_gain.reshape(1, CH)
    x, g = features.reshape(-1, CH), out_grad.reshape(-1, CH)
    xg = (x, *from_ring(x, False))
    og = (g, *from_ring(g, True))
    xin, pre, hid, nrm = front(sizes, xg, conv_weight, gain)
    theirs, ctx, *grads = back(
        sizes, og, xin, hid, nrm, pre, gain, query_weight, key_weight, value_weight, out_weight
    )
    count = lax.axis_size("dp")
    other = lax.ppermute(theirs, "dp", [(i, i ^ 1) for i in range(count)])
    block, mine = rest(sizes, ctx, hid, out_weight, *grads)
    both = (mine.astype(f32) + other.astype(f32)).astype(bf16)
    groups = [[c + 2 * i for i in range(count // 2)] for c in range(2)]
    pieces = lax.all_to_all(both, "dp", 0, 0, tiled=True, axis_index_groups=groups)
    conv_t, *grads = last(pieces)
    return (block.reshape(features.shape), conv_t.T, *grads)


def solution(mesh):
    tiles = P("dp", "sy", "sx", None)
    grad = P("dp", ("sy", "sx"))
    return jax.shard_map(
        body,
        mesh=mesh,
        in_specs=(tiles, P("dp"), P(), P(), P(), P(), P(), P(), P(), tiles),
        out_specs=(tiles, grad, grad, grad, grad, grad),
        check_vma=False,
    )
```
